128 devices in a mesh: section: 2 (over z_lo), dp: 16 (over y, z_hi, core), tensor: 4 (over x).
Axes of the slice: x: 4, y: 4, z: 4 (z_hi: 2, z_lo: 2; z = z_hi * 2 + z_lo), core: 2. Of those that a mesh axis runs over, the one named last changes fastest.
Arguments:
- hidden_parts: bfloat16 [2, 4, 512, 8192], P('section', None, 'dp'), may hold values from -1 to 1
- targets: int32 [4, 512], P(None, 'dp'), may hold values from 0 to 32767
- norm_gain: float32 [8192], replicated, may hold values from 0.1 to 1.9
- head_weight: bfloat16 [8192, 32768], P('dp', ('section', 'tensor')), may hold values from -0.1105957 to 0.1105957
Outputs:
- token_loss: float32 [4, 512], P(None, 'dp')
- hidden_grad: float32 [2, 4, 512, 8192], P('section', None, 'dp')
- head_grad: float32 [8192, 32768], P('dp', ('section', 'tensor'))
- gain_grad: float32 [16, 8192], P('dp')
The draws below stay inside these ranges and needn't reach their ends.
All inputs are finite; a program needn't handle non-finite values.
Results may differ from the reference program's by a relative error of at most 0.0034.
Values may be sent and summed in bfloat16 or wider, within the bound.
No kernel may reach another device: no remote copies, remote signals or barrier semaphores. Data moves between devices by JAX's collectives and lax.ppermute only.
A program may use at most 128 MiB of HBM per device.

```python
import math
import jax
import jax.numpy as jnp
import numpy as np
from jax import lax

D = 8192
MICRO = 4
TOK = 32
TOKENS = 512
VOCAB = 32768
N_SECTION = 2
N_DP = 16


def draw_hidden_parts(key, part):
    key = jax.random.fold_in(key, 11)
    values = jnp.clip(0.25 * jax.random.normal(key, (N_SECTION, MICRO, TOKENS, D), jnp.float32), -1.0, 1.0)
    return values.astype(jnp.bfloat16)


def draw_head_weight(key, part):
    key = jax.random.fold_in(key, 12)
    bound = 3.0 * math.sqrt(3.0 / D)
    values = jax.random.uniform(key, (D, VOCAB), jnp.float32, -bound, bound)
    return values.astype(jnp.bfloat16)


def with_ends(values, key, least, top_value):
    shape = values.shape
    index_at = [jax.random.randint(jax.random.fold_in(key, axis), (), 0, shape[axis]) for axis in range(len(shape))]
    values = values.at[tuple(index_at)].set(least)
    longest = shape.index(max(shape))
    index_at[longest] = (index_at[longest] + 1) % shape[longest]
    return values.at[tuple(index_at)].set(top_value)


def rank_table(amount, lean):
    loads = [(1 << 20) // math.isqrt(standing ** lean) + 1 for standing in range(1, amount + 1)]
    spread = 1 + sum(loads) // (1 << 30)
    return np.cumsum(np.array([max(1, weight // spread) for weight in loads]))


def ranked_ids(own_key, dims, number_of, slope):
    table = rank_table(number_of, slope)
    pick = jax.random.randint(jax.random.fold_in(own_key, 1), dims, 0, int(table[number_of - 1]))
    standing = jnp.searchsorted(jnp.asarray(table, jnp.int32), pick, side="right")
    return jax.random.permutation(jax.random.fold_in(own_key, 2), number_of)[standing].astype(jnp.int32)


def setup_inputs(seed: int = 0) -> dict:
    key_of = jax.random.split(jax.random.key(seed), 5)
    hidden_parts = draw_hidden_parts(jax.random.fold_in(key_of[4], 71), 0)
    targets = with_ends(ranked_ids(key_of[1], (MICRO, TOKENS), VOCAB, 2), jax.random.fold_in(key_of[1], 3), 0, VOCAB - 1).astype(jnp.int32)
    norm_gain = jnp.clip(1.0 + 0.18 * jax.random.normal(key_of[2], (D,), jnp.float32), 0.1, 1.9)
    head_weight = draw_head_weight(jax.random.fold_in(key_of[4], 71), 0)
    return dict(hidden_parts=hidden_parts, targets=targets, norm_gain=norm_gain, head_weight=head_weight)


NORM_EPS = 1e-05

def reference(hidden_parts, targets, norm_gain, head_weight):
    mixed = hidden_parts[0].astype(jnp.float32) + hidden_parts[1].astype(jnp.float32)
    radius = jnp.sqrt(lax.optimization_barrier(jnp.mean(mixed * mixed, axis=-1, keepdims=True)) + NORM_EPS)
    unit_rows = mixed / radius
    normed = (norm_gain * unit_rows).astype(jnp.bfloat16)
    vocab_ids = lax.broadcasted_iota(jnp.int32, (TOKENS, VOCAB), 1)
    head_grad = jnp.zeros((D, VOCAB), jnp.float32)
    losses = []
    grads = []
    for mb_index in range(MICRO):
        rows_now = normed[mb_index]
        logits = jnp.dot(rows_now, head_weight, preferred_element_type=jnp.float32)
        highest = lax.optimization_barrier(jnp.max(logits, axis=1, keepdims=True))
        log_total = highest[:, 0] + jnp.log(lax.optimization_barrier(jnp.sum(jnp.exp(logits - highest), axis=1)))
        is_target = vocab_ids == targets[mb_index].astype(jnp.int32)[:, None]
        target_logit = lax.optimization_barrier(jnp.sum(jnp.where(is_target, logits, jnp.zeros_like(logits)), axis=1))
        losses.append(log_total - target_logit)
        logit_grad = (jnp.exp(logits - log_total[:, None]) - is_target.astype(jnp.float32)).astype(jnp.bfloat16)
        row_grads = lax.dot_general(logit_grad, head_weight, (((1,), (1,)), ((), ())), preferred_element_type=jnp.float32)
        head_grad = head_grad + lax.dot_general(rows_now, logit_grad, (((0,), (0,)), ((), ())), preferred_element_type=jnp.float32)
        grads.append(row_grads)
    token_loss = jnp.stack(losses)
    row_grads = jnp.stack(grads)
    scaled = norm_gain * row_grads
    part_grad = (scaled - unit_rows * lax.optimization_barrier(jnp.mean(scaled * unit_rows, axis=-1, keepdims=True))) / radius
    gain_terms = lax.optimization_barrier(jnp.sum(row_grads * unit_rows, axis=0))
    gain_grad = lax.optimization_barrier(jnp.sum(gain_terms.reshape(N_DP, TOK, D), axis=1))
    return (token_loss, jnp.stack([part_grad, part_grad]), head_grad, gain_grad)
```

```python
import jax
import jax.numpy as jnp
from jax import lax
from jax.sharding import Mesh, PartitionSpec as P

NORM_EPS = 1e-05
CHUNKS = 2
ROW_SCALE = 2.0**17
HEAD_SCALE = 2.0**-3
BF16, F16, F32 = jnp.bfloat16, jnp.float16, jnp.float32


def shift(x, axis, step):
    size = lax.axis_size(axis)
    return lax.ppermute(x, axis, [((i + step) % size, i) for i in range(size)])


def flip(x, axes, bits):
    size = 1
    for axis in axes:
        size *= lax.axis_size(axis)
    return lax.ppermute(x, axes, [(i, i ^ bits) for i in range(size)])


def pick(pieces, index):
    return lax.dynamic_index_in_dim(jnp.stack(pieces), index, 0, keepdims=False)


def merge(parts):
    top = parts[0][..., 0, :]
    for part in parts[1:]:
        top = jnp.maximum(top, part[..., 0, :])
    totals = [part[..., 1, :] * jnp.exp(part[..., 0, :] - top) for part in parts]
    hits = [part[..., 2, :] for part in parts]
    while len(totals) > 1:
        half = len(totals) // 2
        totals = [totals[i] + totals[i + half] for i in range(half)]
        hits = [hits[i] + hits[i + half] for i in range(half)]
    return jnp.stack([top, totals[0], hits[0]], axis=-2)


def local(hidden_parts, targets, norm_gain, head_weight):
    s, y, h, c, t = (lax.axis_index(name) for name in ("s", "y", "h", "c", "t"))
    me = 2 * h + c
    zs = 2 * s + h
    rows, cols = head_weight.shape
    part = cols // 4
    width = 4 * rows
    batches, tok_count, features = hidden_parts.shape[1:]
    count = batches * tok_count
    size = count // CHUNKS
    quarter = size // 4
    eighth = quarter // 2

    blocks = head_weight.reshape(rows, 4, part)
    pieces = [lax.dynamic_index_in_dim(blocks, me ^ r, 1, keepdims=False) for r in range(4)]
    arrived = [pieces[0]] + [flip(pieces[r], ("h", "c"), r) for r in range(1, 4)]
    weight = jnp.concatenate([pick(arrived, me ^ a) for a in range(4)], axis=0)
    first_column = ((2 * h + c) + 4 * (4 * s + t)) * part

    ids = targets.reshape(count)
    ids = [[ids, flip(ids, ("h",), 1)]]
    ids = ids + [[flip(v, ("c",), 1) for v in ids[0]]]

    hidden = hidden_parts.reshape(CHUNKS, 4, quarter, features)

    def normed_rows(k):
        own = lax.dynamic_index_in_dim(hidden[k], t, 0, keepdims=False)
        mixed = own.astype(F32) + flip(own, ("s",), 1).astype(F32)
        radius = jnp.sqrt(jnp.mean(mixed * mixed, axis=-1, keepdims=True) + NORM_EPS)
        unit = mixed / radius
        normed = (norm_gain * unit).astype(BF16)
        sent = [lax.dynamic_slice_in_dim(normed, ((y + r) % 4) * width, width, 1) for r in range(4)]
        over_y = [sent[0]] + [shift(sent[4 - r], "y", r) for r in range(1, 4)]
        over_y = jnp.stack(over_y)
        over_h = jnp.stack([over_y, flip(over_y, ("s", "h"), 3)], axis=1)
        over_t = jnp.stack([over_h] + [shift(over_h, "t", r) for r in range(1, 4)], axis=1)
        over_c = jnp.stack([over_t, flip(over_t, ("c",), 1)], axis=1)
        return unit, radius, over_c.reshape(4, 4 * size, width)

    def logit_rows(k, gathered):
        def product(r):
            return jnp.dot(gathered[r], weight, preferred_element_type=F32)

        out = {r: product(r).astype(F16) for r in (2, 1, 3)}
        own = product(0)
        got = {r: shift(out[(4 - r) % 4], "y", r) for r in (2, 1, 3)}
        return (own + got[2].astype(F32)) + (got[1].astype(F32) + got[3].astype(F32))

    def chunk_ids(k):
        rc_list = []
        for rc in range(2):
            per_h = [ids[rc][rh].reshape(CHUNKS, 4, quarter)[k] for rh in range(2)]
            rolled = []
            for rt in range(4):
                for rh in range(2):
                    rolled.append(lax.dynamic_index_in_dim(per_h[rh], (t + rt) % 4, 0, keepdims=False))
            rc_list.append(jnp.concatenate(rolled))
        return jnp.concatenate(rc_list)

    def loss_and_grad(k, logits):
        is_target = lax.broadcasted_iota(jnp.int32, logits.shape, 1) == (chunk_ids(k) - first_column)[:, None]
        top = jnp.max(logits, axis=1)
        total = jnp.sum(jnp.exp(logits - top[:, None]), axis=1)
        hit = jnp.sum(jnp.where(is_target, logits, 0.0), axis=1)
        stats = jnp.stack([v.reshape(2, 4, 2, quarter) for v in (top, total, hit)], axis=3)
        stats = merge([stats, flip(stats, ("c",), 1)[::-1]])
        got = [flip(stats, ("s", "h"), r) for r in range(1, 4)]
        stats = merge([stats, got[0][:, :, ::-1], got[1], got[2][:, :, ::-1]])
        stats = merge([stats] + [jnp.roll(shift(stats, "t", r), r, axis=1) for r in range(1, 4)])
        log_total = stats[..., 0, :] + jnp.log(stats[..., 1, :])
        loss = log_total - stats[..., 2, :]
        log_total = log_total.reshape(-1)
        grad = (jnp.exp(logits - log_total[:, None]) - is_target.astype(F32)).astype(BF16)
        own = loss[0, :, 0]
        own = jnp.concatenate([lax.dynamic_index_in_dim(own, (a - t) % 4, 0, keepdims=False) for a in range(4)])
        return own, [grad] + [shift(grad, "y", r) for r in range(1, 4)]

    def row_pass(k, unit, radius, grads):
        products = [
            lax.dot_general(g, weight, (((1,), (1,)), ((), ())), preferred_element_type=F32) * ROW_SCALE
            for g in grads
        ]
        half = products[0].shape[0] // 2
        sent = jnp.stack([p[half:].astype(F16) for p in products])
        kept = jnp.stack([p[:half] for p in products]) + flip(sent, ("c",), 1).astype(F32)
        kept = kept.reshape(4, 4, 2 * quarter, width)
        sent = kept[:, 1:].astype(F16)
        got = [shift(sent[:, (4 - r) - 1], "t", r) for r in range(1, 4)]
        kept = (kept[:, 0] + got[1].astype(F32)) + (got[0].astype(F32) + got[2].astype(F32))
        kept = kept.reshape(4, 2, 2, eighth, width)
        mine = lax.dynamic_index_in_dim(kept, s, 2, keepdims=False)
        other = lax.dynamic_index_in_dim(kept, 1 - s, 2, keepdims=False).astype(F16)
        got = [
            flip(mine[:, 1].astype(F16), ("s", "h"), 1),
            flip(other[:, 0], ("s", "h"), 2),
            flip(other[:, 1], ("s", "h"), 3),
        ]
        summed = (mine[:, 0] + got[0].astype(F32)) + (got[1].astype(F32) + got[2].astype(F32))
        summed16 = summed.astype(F16)
        over_y = [summed] + [shift(summed16[4 - r], "y", r).astype(F32) for r in range(1, 4)]
        over_y[0] = summed[0]
        row_grads = jnp.concatenate(
            [pick(over_y, (b - y) % 4) for b in range(4)], axis=1
        ) * (1.0 / ROW_SCALE)
        unit = lax.dynamic_slice_in_dim(unit, s * eighth, eighth, 0)
        radius = lax.dynamic_slice_in_dim(radius, s * eighth, eighth, 0)
        scaled = norm_gain * row_grads
        hidden_grad = (scaled - unit * jnp.mean(scaled * unit, axis=-1, keepdims=True)) / radius
        gain_part = jnp.sum(row_grads * unit, axis=0, keepdims=True)
        mine = hidden_grad.astype(BF16)
        got = flip(mine, ("s",), 1)
        pair = jnp.stack([pick([mine, got], a ^ s) for a in range(2)]).reshape(quarter, features)
        all_t = [pair] + [shift(pair, "t", r) for r in range(1, 4)]
        rows_out = jnp.concatenate([pick(all_t, (a - t) % 4) for a in range(4)], axis=0).astype(F32)
        return rows_out, gain_part

    def head_part(gathered, grads):
        all_grads = jnp.concatenate(grads, axis=0)
        return lax.dot_general(
            gathered.reshape(-1, width), all_grads, (((0,), (0,)), ((), ())), preferred_element_type=F32
        )

    stage = [normed_rows(k) for k in range(CHUNKS)]
    logits = [logit_rows(k, stage[k][2]) for k in range(CHUNKS)]
    graded = [loss_and_grad(k, logits[k]) for k in range(CHUNKS)]
    head = head_part(stage[0][2], graded[0][1])
    for k in range(1, CHUNKS):
        head = head + head_part(stage[k][2], graded[k][1])
    rows_done = [row_pass(k, stage[k][0], stage[k][1], graded[k][1]) for k in range(CHUNKS)]

    head = head.reshape(4, rows, part)
    head_grad = jnp.zeros((rows, cols), F32)
    for r in range(4):
        piece = lax.dynamic_index_in_dim(head, me ^ r, 0, keepdims=False)
        if r:
            piece = flip((piece * HEAD_SCALE).astype(F16), ("h", "c"), r).astype(F32) * (1.0 / HEAD_SCALE)
        head_grad = lax.dynamic_update_slice(head_grad, piece, (0, (me ^ r) * part))

    gain = sum(r[1] for r in rows_done)
    gain = gain + flip(gain, ("s",), 1)
    gains = [gain] + [shift(gain, "t", r) for r in range(1, 4)]
    gain = (gains[0] + gains[2]) + (gains[1] + gains[3])
    token_loss = jnp.concatenate([g[0] for g in graded]).reshape(batches, tok_count)
    hidden_grad = jnp.concatenate([r[0] for r in rows_done]).reshape(1, batches, tok_count, features)
    return token_loss, hidden_grad, head_grad, gain


def solution(mesh):
    fine = Mesh(mesh.devices.reshape(2, 4, 2, 2, 4), ("s", "y", "h", "c", "t"))
    dp = ("y", "h", "c")
    in_specs = (P("s", None, dp, None), P(None, dp), P(), P(dp, ("s", "t")))
    out_specs = (P(None, dp), P("s", None, dp, None), P(dp, ("s", "t")), P(dp, None))
    return jax.shard_map(local, mesh=fine, in_specs=in_specs, out_specs=out_specs, check_vma=False)
```

```python
import jax
import jax.numpy as jnp
from jax import lax
from jax.sharding import Mesh, PartitionSpec as P

NORM_EPS = 1e-05
CHUNKS = 2
ROW_SCALE = 2.0**17
HEAD_SCALE = 2.0**-3
BF16, F16, F32 = jnp.bfloat16, jnp.float16, jnp.float32


def shift(x, axis, step):
    size = lax.axis_size(axis)
    return lax.ppermute(x, axis, [((i + step) % size, i) for i in range(size)])


def flip(x, axes, bits):
    size = 1
    for axis in axes:
        size *= lax.axis_size(axis)
    return lax.ppermute(x, axes, [(i, i ^ bits) for i in range(size)])


def after(x, y):
    return lax.optimization_barrier((x, y))[0]


def pick(pieces, index):
    return lax.dynamic_index_in_dim(jnp.stack(pieces), index, 0, keepdims=False)


def merge(parts):
    top = parts[0][..., 0, :]
    for part in parts[1:]:
        top = jnp.maximum(top, part[..., 0, :])
    totals = [part[..., 1, :] * jnp.exp(part[..., 0, :] - top) for part in parts]
    hits = [part[..., 2, :] for part in parts]
    while len(totals) > 1:
        half = len(totals) // 2
        totals = [totals[i] + totals[i + half] for i in range(half)]
        hits = [hits[i] + hits[i + half] for i in range(half)]
    return jnp.stack([top, totals[0], hits[0]], axis=-2)


def local(hidden_parts, targets, norm_gain, head_weight):
    s, y, h, c, t = (lax.axis_index(name) for name in ("s", "y", "h", "c", "t"))
    me = 2 * h + c
    rows, cols = head_weight.shape
    part = cols // 4
    width = 4 * rows
    batches, tok_count, features = hidden_parts.shape[1:]
    count = batches * tok_count
    size = count // CHUNKS
    quarter = size // 4
    eighth = quarter // 2

    pieces = [lax.dynamic_slice_in_dim(head_weight, (me ^ r) * part, part, 1) for r in range(4)]
    arrived = [pieces[0]] + [flip(pieces[r], ("h", "c"), r) for r in range(1, 4)]
    weight = jnp.concatenate([pick(arrived, me ^ a) for a in range(4)], axis=0)
    first_column = (me + 4 * (4 * s + t)) * part

    hidden = hidden_parts.reshape(CHUNKS, 4, quarter, features)
    own = lax.dynamic_index_in_dim(hidden, t, 1, keepdims=False).reshape(CHUNKS * quarter, features)
    mixed = own.astype(F32) + flip(own, ("s",), 1).astype(F32)
    radius = jnp.sqrt(jnp.mean(mixed * mixed, axis=-1, keepdims=True) + NORM_EPS)
    unit = mixed / radius
    normed = after((norm_gain * unit).astype(BF16), arrived[2])
    sent = [lax.dynamic_slice_in_dim(normed, ((y + r) % 4) * width, width, 1) for r in range(4)]
    over_y = [sent[0]] + [shift(sent[4 - r], "y", r) for r in range(1, 4)]
    over_y = jnp.stack([v.reshape(CHUNKS, quarter, width) for v in over_y], axis=1)
    over_h = jnp.stack([over_y, flip(over_y, ("s", "h"), 3)], axis=2)
    unit = unit.reshape(CHUNKS, 2, eighth, features)
    radius = radius.reshape(CHUNKS, 2, eighth, 1)

    ids = after(targets.reshape(count), over_y)
    ids = [[ids, flip(ids, ("h",), 1)]]
    ids = ids + [[flip(v, ("c",), 1) for v in ids[0]]]

    def gather(k):
        over_t = jnp.stack([over_h[k]] + [shift(over_h[k], "t", r) for r in range(1, 4)], axis=1)
        over_c = jnp.stack([over_t, flip(over_t, ("c",), 1)], axis=1)
        return over_c.reshape(4, 4 * size, width)

    def partial_logits(gathered):
        out = {r: jnp.dot(gathered[r], weight, preferred_element_type=F32).astype(F16) for r in (2, 1, 3)}
        own = jnp.dot(gathered[0], weight, preferred_element_type=F32)
        return own, {r: shift(out[4 - r], "y", r) for r in (2, 1, 3)}

    def chunk_ids(k):
        listed = []
        for rc in range(2):
            per_h = [ids[rc][rh].reshape(CHUNKS, 4, quarter)[k] for rh in range(2)]
            for rt in range(4):
                for rh in range(2):
                    listed.append(lax.dynamic_index_in_dim(per_h[rh], (t + rt) % 4, 0, keepdims=False))
        return jnp.concatenate(listed)

    def loss_and_grad(k, own, got, before_last):
        logits = (own + got[2].astype(F32)) + (got[1].astype(F32) + got[3].astype(F32))
        is_target = lax.broadcasted_iota(jnp.int32, logits.shape, 1) == (chunk_ids(k) - first_column)[:, None]
        top = jnp.max(logits, axis=1)
        total = jnp.sum(jnp.exp(logits - top[:, None]), axis=1)
        hit = jnp.sum(jnp.where(is_target, logits, 0.0), axis=1)
        stats = jnp.stack([v.reshape(2, 4, 2, quarter) for v in (top, total, hit)], axis=3)
        stats = merge([stats, flip(stats, ("c",), 1)[::-1]])
        got = [flip(stats, ("s", "h"), r) for r in range(1, 4)]
        stats = merge([stats, got[0][:, :, ::-1], got[1], got[2][:, :, ::-1]])
        if before_last is not None:
            stats = after(stats, before_last)
        stats = merge([stats] + [jnp.roll(shift(stats, "t", r), r, axis=1) for r in range(1, 4)])
        log_total = stats[..., 0, :] + jnp.log(stats[..., 1, :])
        loss = log_total - stats[..., 2, :]
        log_total = log_total.reshape(-1)
        grad = (jnp.exp(logits - log_total[:, None]) - is_target.astype(F32)).astype(BF16)
        own = loss[0, :, 0]
        own = jnp.concatenate([lax.dynamic_index_in_dim(own, (a - t) % 4, 0, keepdims=False) for a in range(4)])
        return own, [grad] + [shift(grad, "y", r) for r in range(1, 4)]

    def row_products(grads):
        return [
            lax.dot_general(g, weight, (((1,), (1,)), ((), ())), preferred_element_type=F32) * ROW_SCALE
            for g in grads
        ]

    def head_product(gathered, grads):
        return lax.dot_general(
            gathered.reshape(-1, width),
            jnp.concatenate(grads, axis=0),
            (((0,), (0,)), ((), ())),
            preferred_element_type=F32,
        )

    def over_cores(products, wait):
        half = products[0].shape[0] // 2
        sent = jnp.stack([p[half:].astype(F16) for p in products])
        if wait is not None:
            sent = after(sent, wait)
        kept = jnp.stack([p[:half] for p in products]) + flip(sent, ("c",), 1).astype(F32)
        return kept.reshape(4, 4, 2 * quarter, width)

    def over_tensor(kept):
        sent = kept[:, 1:].astype(F16)
        got = [shift(sent[:, 3 - r], "t", r).astype(F32) for r in range(1, 4)]
        kept = (kept[:, 0] + got[1]) + (got[0] + got[2])
        return kept.reshape(4, 2, 2, eighth, width)

    def over_z(kept):
        mine = lax.dynamic_index_in_dim(kept, s, 2, keepdims=False)
        other = lax.dynamic_index_in_dim(kept, 1 - s, 2, keepdims=False).astype(F16)
        got = [
            flip(mine[:, 1].astype(F16), ("s", "h"), 1).astype(F32),
            flip(other[:, 0], ("s", "h"), 2).astype(F32),
            flip(other[:, 1], ("s", "h"), 3).astype(F32),
        ]
        return (mine[:, 0] + got[0]) + (got[1] + got[2])

    def to_owner(k, summed):
        sent = summed.astype(F16)
        blocks = [summed[0]] + [shift(sent[4 - r], "y", r).astype(F32) for r in range(1, 4)]
        row_grads = jnp.concatenate([pick(blocks, (b - y) % 4) for b in range(4)], axis=1) * (1.0 / ROW_SCALE)
        u = lax.dynamic_index_in_dim(unit[k], s, 0, keepdims=False)
        scaled = norm_gain * row_grads
        hidden_grad = scaled - u * jnp.mean(scaled * u, axis=-1, keepdims=True)
        hidden_grad = hidden_grad / lax.dynamic_index_in_dim(radius[k], s, 0, keepdims=False)
        return hidden_grad.astype(BF16), jnp.sum(row_grads * u, axis=0, keepdims=True)

    def to_all(mine):
        got = flip(mine, ("s",), 1)
        pair = jnp.stack([pick([mine, got], a ^ s) for a in range(2)]).reshape(quarter, features)
        all_t = [pair] + [shift(pair, "t", r) for r in range(1, 4)]
        return jnp.concatenate([pick(all_t, (a - t) % 4) for a in range(4)], axis=0).astype(F32)

    x0 = gather(0)
    own0, got0 = partial_logits(x0)
    x1 = gather(1)
    own1, got1 = partial_logits(x1)
    loss0, grads0 = loss_and_grad(0, own0, got0, None)
    own1 = after(own1, grads0[0])
    loss1, grads1 = loss_and_grad(1, own1, got1, grads0[1])

    rows0 = over_tensor(over_cores(row_products(grads0), None))
    head0 = head_product(x0, grads0)
    grads1 = [after(grads1[0], head0)] + grads1[1:]
    kept1 = over_cores(row_products(grads1), rows0)
    head = head0 + head_product(x1, after(grads1, kept1[0, 0, 0, 0]))
    head = head.reshape(4, rows, part)
    got_head = [lax.dynamic_index_in_dim(head, me, 0, keepdims=False)]
    for r in range(1, 4):
        piece = lax.dynamic_index_in_dim(head, me ^ r, 0, keepdims=False)
        got_head.append(flip((piece * HEAD_SCALE).astype(F16), ("h", "c"), r))
    summed0 = over_z(rows0)
    rows1 = over_tensor(kept1)
    hid0, gain0 = to_owner(0, summed0)
    summed1 = over_z(after(rows1, hid0))
    out0 = to_all(after(hid0, rows1))
    hid1, gain1 = to_owner(1, summed1)
    out1 = to_all(after(hid1, out0))

    gain = gain0 + gain1
    gain = gain + flip(gain, ("s",), 1)
    gains = [gain] + [shift(gain, "t", r) for r in range(1, 4)]
    gain = (gains[0] + gains[2]) + (gains[1] + gains[3])

    head_grad = jnp.zeros((rows, cols), F32)
    for r in range(4):
        piece = got_head[r]
        if r:
            piece = after(piece, hid1).astype(F32) * (1.0 / HEAD_SCALE)
        head_grad = lax.dynamic_update_slice(head_grad, piece, (0, (me ^ r) * part))

    token_loss = jnp.concatenate([loss0, loss1]).reshape(batches, tok_count)
    hidden_grad = jnp.concatenate([out0, out1]).reshape(1, batches, tok_count, features)
    return token_loss, hidden_grad, head_grad, gain


def solution(mesh):
    fine = Mesh(mesh.devices.reshape(2, 4, 2, 2, 4), ("s", "y", "h", "c", "t"))
    dp = ("y", "h", "c")
    in_specs = (P("s", None, dp, None), P(None, dp), P(), P(dp, ("s", "t")))
    out_specs = (P(None, dp), P("s", None, dp, None), P(dp, ("s", "t")), P(dp, None))
    return jax.shard_map(local, mesh=fine, in_specs=in_specs, out_specs=out_specs, check_vma=False)
```

```python
import jax
import jax.numpy as jnp
from jax import lax
from jax.sharding import Mesh, PartitionSpec as P

NORM_EPS = 1e-05
CHUNKS = 2
ROW_SCALE = 2.0**17
HEAD_SCALE = 2.0**-3
BF16, F16, F32 = jnp.bfloat16, jnp.float16, jnp.float32


def shift(x, axis, step):
    size = lax.axis_size(axis)
    return lax.ppermute(x, axis, [((i + step) % size, i) for i in range(size)])


def flip(x, axes, bits):
    size = 1
    for axis in axes:
        size *= lax.axis_size(axis)
    return lax.ppermute(x, axes, [(i, i ^ bits) for i in range(size)])


def after(x, y):
    return lax.optimization_barrier((x, y))[0]


def pick(pieces, index):
    return lax.dynamic_index_in_dim(jnp.stack(pieces), index, 0, keepdims=False)


def merge(parts):
    top = parts[0][..., 0, :]
    for part in parts[1:]:
        top = jnp.maximum(top, part[..., 0, :])
    totals = [part[..., 1, :] * jnp.exp(part[..., 0, :] - top) for part in parts]
    hits = [part[..., 2, :] for part in parts]
    while len(totals) > 1:
        half = len(totals) // 2
        totals = [totals[i] + totals[i + half] for i in range(half)]
        hits = [hits[i] + hits[i + half] for i in range(half)]
    return jnp.stack([top, totals[0], hits[0]], axis=-2)


def local(hidden_parts, targets, norm_gain, head_weight):
    s, y, h, c, t = (lax.axis_index(name) for name in ("s", "y", "h", "c", "t"))
    me = 2 * h + c
    rows, cols = head_weight.shape
    part = cols // 4
    width = 4 * rows
    batches, tok_count, features = hidden_parts.shape[1:]
    count = batches * tok_count
    size = count // CHUNKS
    quarter = size // 4
    eighth = quarter // 2

    pieces = [lax.dynamic_slice_in_dim(head_weight, (me ^ r) * part, part, 1) for r in range(4)]
    arrived = [pieces[0], flip(pieces[1], ("h", "c"), 1), flip(pieces[2], ("h", "c"), 2)]
    first_column = (me + 4 * (4 * s + t)) * part

    hidden = hidden_parts.reshape(CHUNKS, 4, quarter, features)
    own = lax.dynamic_index_in_dim(hidden, t, 1, keepdims=False).reshape(CHUNKS * quarter, features)
    mixed = own.astype(F32) + flip(own, ("s",), 1).astype(F32)
    radius = jnp.sqrt(jnp.mean(mixed * mixed, axis=-1, keepdims=True) + NORM_EPS)
    unit = mixed / radius
    normed = (norm_gain * unit).astype(BF16)
    sent = [lax.dynamic_slice_in_dim(normed, ((y + r) % 4) * width, width, 1) for r in range(4)]
    sent[2] = after(sent[2], arrived[2])
    over_y = [sent[0]] + [shift(sent[4 - r], "y", r) for r in range(1, 4)]
    over_y = jnp.stack([v.reshape(CHUNKS, quarter, width) for v in over_y], axis=1)
    got = flip(over_y, ("s", "h"), 3)
    over_h = jnp.stack([over_y, got], axis=2)
    arrived.append(flip(after(pieces[3], got), ("h", "c"), 3))
    weight = jnp.concatenate([pick(arrived, me ^ a) for a in range(4)], axis=0)
    unit = unit.reshape(CHUNKS, 2, eighth, features)
    radius = radius.reshape(CHUNKS, 2, eighth, 1)

    ids = after(targets.reshape(count), over_y)
    ids = jnp.stack([ids, flip(ids, ("h",), 1)])
    ids = [ids, flip(ids, ("c",), 1)]

    def gather(k, wait):
        got = after([shift(over_h[k], "t", r) for r in range(1, 4)], wait)
        over_t = jnp.stack([over_h[k]] + got, axis=1)
        over_c = jnp.stack([over_t, flip(over_t, ("c",), 1)], axis=1)
        return over_c.reshape(4, 4 * size, width)

    def partial_logits(gathered):
        out = {r: jnp.dot(gathered[r], weight, preferred_element_type=F32).astype(F16) for r in (2, 1, 3)}
        own = jnp.dot(gathered[0], weight, preferred_element_type=F32)
        return own, {r: shift(out[4 - r], "y", r) for r in (2, 1, 3)}, [out[r] for r in (1, 2, 3)]

    def chunk_ids(k):
        listed = []
        for rc in range(2):
            per_h = [ids[rc][rh].reshape(CHUNKS, 4, quarter)[k] for rh in range(2)]
            for rt in range(4):
                for rh in range(2):
                    listed.append(lax.dynamic_index_in_dim(per_h[rh], (t + rt) % 4, 0, keepdims=False))
        return jnp.concatenate(listed)

    def loss_and_grad(k, own, got, before_last):
        logits = (own + got[2].astype(F32)) + (got[1].astype(F32) + got[3].astype(F32))
        is_target = lax.broadcasted_iota(jnp.int32, logits.shape, 1) == (chunk_ids(k) - first_column)[:, None]
        top = jnp.max(logits, axis=1)
        total = jnp.sum(jnp.exp(logits - top[:, None]), axis=1)
        hit = jnp.sum(jnp.where(is_target, logits, 0.0), axis=1)
        stats = jnp.stack([v.reshape(2, 4, 2, quarter) for v in (top, total, hit)], axis=3)
        stats = merge([stats, flip(stats, ("c",), 1)[::-1]])
        got = [flip(stats, ("s", "h"), r) for r in range(1, 4)]
        stats = merge([stats, got[0][:, :, ::-1], got[1], got[2][:, :, ::-1]])
        if before_last is not None:
            stats = after(stats, before_last)
        stats = merge([stats] + [jnp.roll(shift(stats, "t", r), r, axis=1) for r in range(1, 4)])
        log_total = stats[..., 0, :] + jnp.log(stats[..., 1, :])
        loss = log_total - stats[..., 2, :]
        log_total = log_total.reshape(-1)
        grad = (jnp.exp(logits - log_total[:, None]) - is_target.astype(F32)).astype(BF16)
        own = loss[0, :, 0]
        own = jnp.concatenate([lax.dynamic_index_in_dim(own, (a - t) % 4, 0, keepdims=False) for a in range(4)])
        return own, [grad] + [shift(grad, "y", r) for r in range(1, 4)]

    def row_products(grads):
        return [
            lax.dot_general(g, weight, (((1,), (1,)), ((), ())), preferred_element_type=F32) * ROW_SCALE
            for g in grads
        ]

    def head_product(gathered, grads):
        return lax.dot_general(
            gathered.reshape(-1, width),
            jnp.concatenate(grads, axis=0),
            (((0,), (0,)), ((), ())),
            preferred_element_type=F32,
        )

    def over_cores(products, wait):
        half = products[0].shape[0] // 2
        sent = jnp.stack([p[half:].astype(F16) for p in products])
        got = flip(after(sent, wait), ("c",), 1)
        kept = jnp.stack([p[:half] for p in products]) + got.astype(F32)
        return kept.reshape(4, 4, 2 * quarter, width)

    def over_tensor(kept):
        sent = kept[:, 1:].astype(F16)
        got = [shift(sent[:, 3 - r], "t", r) for r in range(1, 4)]
        kept = (kept[:, 0] + got[1].astype(F32)) + (got[0].astype(F32) + got[2].astype(F32))
        return kept.reshape(4, 2, 2, eighth, width), got

    def over_z(kept):
        mine = lax.dynamic_index_in_dim(kept, s, 2, keepdims=False)
        other = lax.dynamic_index_in_dim(kept, 1 - s, 2, keepdims=False).astype(F16)
        got = [
            flip(mine[:, 1].astype(F16), ("s", "h"), 1),
            flip(other[:, 0], ("s", "h"), 2),
            flip(other[:, 1], ("s", "h"), 3),
        ]
        return (mine[:, 0] + got[0].astype(F32)) + (got[1].astype(F32) + got[2].astype(F32)), got

    def to_owner(k, summed):
        sent = summed.astype(F16)
        got = [shift(sent[4 - r], "y", r) for r in range(1, 4)]
        blocks = [summed[0]] + [g.astype(F32) for g in got]
        row_grads = jnp.concatenate([pick(blocks, (b - y) % 4) for b in range(4)], axis=1) * (1.0 / ROW_SCALE)
        u = lax.dynamic_index_in_dim(unit[k], s, 0, keepdims=False)
        scaled = norm_gain * row_grads
        hidden_grad = scaled - u * jnp.mean(scaled * u, axis=-1, keepdims=True)
        hidden_grad = hidden_grad / lax.dynamic_index_in_dim(radius[k], s, 0, keepdims=False)
        return hidden_grad.astype(BF16), jnp.sum(row_grads * u, axis=0, keepdims=True), got

    def in_order(mine, got):
        return jnp.stack([pick([mine, got], a ^ s) for a in range(2)]).reshape(quarter, features)

    def all_rows(pieces):
        return jnp.concatenate([pick(pieces, (a - t) % 4) for a in range(4)], axis=0).astype(F32)

    def halves(v):
        upper = v.astype(BF16)
        return [upper, (v - upper.astype(F32)).astype(BF16)]

    def whole(rows):
        return rows[-2:-1].astype(F32) + rows[-1:].astype(F32)

    x0 = gather(0, arrived[3])
    own0, got0, last0 = partial_logits(x0)
    x1 = gather(1, last0)
    own1, got1, last1 = partial_logits(x1)
    loss0, grads0 = loss_and_grad(0, after(own0, last1), got0, None)
    loss1, grads1 = loss_and_grad(1, after(own1, grads0[0]), got1, grads0[1])

    rows0, got_t0 = over_tensor(over_cores(row_products(grads0), last1))
    head0 = head_product(x0, grads0)
    summed0, got_z0 = over_z(rows0)
    hid0, gain0, got_y0 = to_owner(0, summed0)
    pair0 = flip(hid0, ("s",), 1)

    grads1 = after(grads1, (head0, got_t0))
    head = (head0 + head_product(x1, grads1)).reshape(4, rows, part)
    pieces = [lax.dynamic_index_in_dim(head, me ^ r, 0, keepdims=False) for r in range(4)]
    sent = [None] + [(piece * HEAD_SCALE).astype(F16) for piece in pieces[1:]]
    got_head = [pieces[0]] + [flip(after(sent[r], pair0), ("h", "c"), r) for r in range(1, 4)]
    kept1 = over_cores(row_products(after(grads1, (sent[2:], got_z0))), got_y0)
    rows1, got_t1 = over_tensor(kept1)
    whole0 = after(in_order(hid0, pair0), got_t1)
    all0 = [whole0] + [shift(whole0, "t", r) for r in range(1, 4)]
    out0 = all_rows(all0)
    hid1, gain1, _ = to_owner(1, over_z(after(rows1, (got_head[2:], all0[1:])))[0])

    sent1 = jnp.concatenate([hid1] + halves(gain0 + gain1), axis=0)
    pair1 = flip(sent1, ("s",), 1)
    whole1 = in_order(hid1, pair1[:eighth])
    whole1 = jnp.concatenate([whole1] + halves(whole(sent1) + whole(pair1)), axis=0)
    all1 = [whole1] + [shift(whole1, "t", r) for r in range(1, 4)]
    out1 = all_rows([v[:quarter] for v in all1])
    gain = (whole(all1[0]) + whole(all1[2])) + (whole(all1[1]) + whole(all1[3]))

    head_grad = jnp.zeros((rows, cols), F32)
    for r in range(4):
        piece = got_head[r]
        if r:
            piece = after(piece, pair1).astype(F32) * (1.0 / HEAD_SCALE)
        head_grad = lax.dynamic_update_slice(head_grad, piece, (0, (me ^ r) * part))

    token_loss = jnp.concatenate([loss0, loss1]).reshape(batches, tok_count)
    hidden_grad = jnp.concatenate([out0, out1]).reshape(1, batches, tok_count, features)
    return token_loss, hidden_grad, head_grad, gain


def solution(mesh):
    fine = Mesh(mesh.devices.reshape(2, 4, 2, 2, 4), ("s", "y", "h", "c", "t"))
    dp = ("y", "h", "c")
    in_specs = (P("s", None, dp, None), P(None, dp), P(), P(dp, ("s", "t")))
    out_specs = (P(None, dp), P("s", None, dp, None), P(dp, ("s", "t")), P(dp, None))
    return jax.shard_map(local, mesh=fine, in_specs=in_specs, out_specs=out_specs, check_vma=False)
```

```python
import jax
import jax.numpy as jnp
from jax import lax
from jax.sharding import Mesh, PartitionSpec as P

NORM_EPS = 1e-05
CHUNKS = 2
ROW_SCALE = 2.0**17
HEAD_SCALE = 2.0**-3
BF16, F16, F32 = jnp.bfloat16, jnp.float16, jnp.float32


def shift(x, axis, step):
    size = lax.axis_size(axis)
    return lax.ppermute(x, axis, [((i + step) % size, i) for i in range(size)])


def flip(x, axes, bits):
    size = 1
    for axis in axes:
        size *= lax.axis_size(axis)
    return lax.ppermute(x, axes, [(i, i ^ bits) for i in range(size)])


def after(x, y):
    return lax.optimization_barrier((x, y))[0]


def merge(parts):
    top = parts[0][..., 0, :]
    for part in parts[1:]:
        top = jnp.maximum(top, part[..., 0, :])
    totals = [part[..., 1, :] * jnp.exp(part[..., 0, :] - top) for part in parts]
    hits = [part[..., 2, :] for part in parts]
    while len(totals) > 1:
        half = len(totals) // 2
        totals = [totals[i] + totals[i + half] for i in range(half)]
        hits = [hits[i] + hits[i + half] for i in range(half)]
    return jnp.stack([top, totals[0], hits[0]], axis=-2)


def swap(x, axis):
    return lax.all_to_all(x, axis, 0, 0, tiled=True)


def total(pieces):
    pieces = pieces.astype(F32)
    return (pieces[0] + pieces[2]) + (pieces[1] + pieces[3])


def local(hidden_parts, targets, norm_gain, head_weight):
    s, h, c, t = (lax.axis_index(name) for name in ("s", "h", "c", "t"))
    me = 2 * h + c
    rows, cols = head_weight.shape
    part = cols // 4
    width = 4 * rows
    batches, tok_count, features = hidden_parts.shape[1:]
    count = batches * tok_count
    size = count // CHUNKS
    quarter = size // 4
    eighth = quarter // 2

    pieces = [lax.dynamic_slice_in_dim(head_weight, (me ^ r) * part, part, 1) for r in range(4)]
    arrived = [pieces[0], flip(pieces[1], ("h", "c"), 1), flip(pieces[2], ("h", "c"), 2)]
    first_column = (me + 4 * (4 * s + t)) * part

    hidden = hidden_parts.reshape(CHUNKS, 4, quarter, features)
    own = lax.dynamic_index_in_dim(hidden, t, 1, keepdims=False).reshape(CHUNKS * quarter, features)
    mixed = own.astype(F32) + flip(own, ("s",), 1).astype(F32)
    radius = jnp.sqrt(jnp.mean(mixed * mixed, axis=-1, keepdims=True) + NORM_EPS)
    unit = mixed / radius
    normed = (norm_gain * unit).astype(BF16)
    over_y = swap(normed.reshape(CHUNKS * quarter, 4, width).transpose(1, 0, 2), "y")
    got = flip(after(over_y, arrived[2]), ("s", "h"), 3)
    arrived.append(flip(after(pieces[3], got), ("h", "c"), 3))
    blocks = jnp.stack(arrived)
    weight = jnp.concatenate([lax.dynamic_index_in_dim(blocks, me ^ a, 0, keepdims=False) for a in range(4)], axis=0)
    over_h = [
        jnp.stack([v.reshape(4, CHUNKS, quarter, width)[:, k] for v in (over_y, got)], axis=1) for k in range(CHUNKS)
    ]
    unit = unit.reshape(CHUNKS, 2, eighth, features)
    radius = radius.reshape(CHUNKS, 2, eighth, 1)

    ids = after(targets.reshape(count), got)
    ids = jnp.stack([ids, flip(ids, ("h",), 1)])
    ids = jnp.stack([ids, flip(ids, ("c",), 1)])

    def gather(k, wait):
        over_t = after(lax.all_gather(over_h[k], "t", axis=0), wait)
        over_c = jnp.stack([over_t, flip(over_t, ("c",), 1)]).transpose(2, 0, 1, 3, 4, 5)
        return lax.optimization_barrier(over_c.reshape(16 * size, width))

    def partial_logits(gathered):
        out = jnp.dot(gathered, weight, preferred_element_type=F32).astype(F16).reshape(4, 4 * size, part)
        return out, swap(out, "y")

    def loss_and_grad(k, pieces, before_last):
        logits = total(pieces)
        here = ids.reshape(2, 2, CHUNKS, 4, quarter)[:, :, k].transpose(0, 2, 1, 3).reshape(-1)
        is_target = lax.broadcasted_iota(jnp.int32, logits.shape, 1) == (here - first_column)[:, None]
        top = jnp.max(logits, axis=1)
        sums = jnp.sum(jnp.exp(logits - top[:, None]), axis=1)
        hit = jnp.sum(jnp.where(is_target, logits, 0.0), axis=1)
        stats = jnp.stack([v.reshape(2, 4, 2, quarter) for v in (top, sums, hit)], axis=3)
        stats = merge([stats, flip(stats, ("c",), 1)[::-1]])
        got = [flip(stats, ("s", "h"), r) for r in range(1, 4)]
        stats = merge([stats, got[0][:, :, ::-1], got[1], got[2][:, :, ::-1]])
        stats = after(stats, before_last)
        stats = merge([stats] + [shift(stats, "t", r) for r in range(1, 4)])
        log_total = stats[..., 0, :] + jnp.log(stats[..., 1, :])
        loss = log_total - stats[..., 2, :]
        grad = (jnp.exp(logits - log_total.reshape(-1)[:, None]) - is_target.astype(F32)).astype(BF16)
        return loss[0, :, 0].reshape(size), grad, lax.all_gather(grad, "y", axis=0, tiled=True)

    def row_product(grads):
        return lax.dot_general(grads, weight, (((1,), (1,)), ((), ())), preferred_element_type=F32) * ROW_SCALE

    def head_product(gathered, grads):
        return lax.dot_general(gathered, grads, (((0,), (0,)), ((), ())), preferred_element_type=F32)

    def over_cores(product, wait):
        product = product.reshape(4, 2, 2 * size, width)
        got = flip(after(product[:, 1].astype(F16), wait), ("c",), 1)
        return product[:, 0] + got.astype(F32)

    def over_tensor(kept):
        sent = kept.reshape(4, 4, 2 * quarter, width).transpose(1, 0, 2, 3).astype(F16)
        return swap(sent, "t")

    def over_z(pieces):
        kept = total(pieces).astype(F16).reshape(4, 2, 2, eighth, width)
        kept = jnp.where(h == 0, kept, kept[:, ::-1]).transpose(2, 1, 0, 3, 4)
        return swap(kept.reshape(4, 4, eighth, width), ("s", "h"))

    def to_owner(k, pieces):
        got = swap(total(pieces).astype(F16), "y")
        row_grads = got.transpose(1, 0, 2).reshape(eighth, features).astype(F32) * (1.0 / ROW_SCALE)
        u = lax.dynamic_index_in_dim(unit[k], s, 0, keepdims=False)
        scaled = norm_gain * row_grads
        hidden_grad = scaled - u * jnp.mean(scaled * u, axis=-1, keepdims=True)
        hidden_grad = hidden_grad / lax.dynamic_index_in_dim(radius[k], s, 0, keepdims=False)
        return hidden_grad.astype(BF16), jnp.sum(row_grads * u, axis=0, keepdims=True), got

    def in_order(everyone):
        everyone = everyone.reshape(2, 4, eighth, features).transpose(1, 0, 2, 3)
        return everyone.reshape(size, features).astype(F32)

    x0 = gather(0, (arrived[3], ids))
    part0, got0 = partial_logits(x0)
    x1 = gather(1, part0)
    part1, got1 = partial_logits(x1)
    loss0, grad0, grads0 = loss_and_grad(0, got0, part1)
    loss1, grad1, grads1 = loss_and_grad(1, after(got1, grad0), grad0)

    got_t0 = over_tensor(over_cores(row_product(grads0), part1))
    head0 = head_product(x0, after(grads0, grad1))
    got_z0 = over_z(got_t0)
    hid0, gain0, got_y0 = to_owner(0, got_z0)

    grads1 = after(grads1, (head0, got_t0))
    head = ((head0 + head_product(x1, grads1)) * HEAD_SCALE).astype(F16).reshape(4, rows, part)
    got_head = [lax.dynamic_index_in_dim(head, me ^ r, 0, keepdims=False) for r in range(4)]
    got_head = [got_head[0]] + [flip(after(got_head[r], got_z0), ("h", "c"), r) for r in range(1, 4)]
    kept1 = over_cores(row_product(after(grads1, (head, got_z0))), got_y0)
    got_t1 = over_tensor(kept1)
    hid1, gain1, _ = to_owner(1, over_z(after(got_t1, got_head[2:])))
    all0 = lax.all_gather(after(hid0, (got_head[2:], got_t1)), ("s", "t"))

    gain = gain0 + gain1
    upper = gain.astype(BF16)
    lower = (gain - upper.astype(F32)).astype(BF16)
    sent = jnp.concatenate([hid1, upper, lower], axis=0)
    all1 = lax.all_gather(sent, ("s", "t"))
    gain = jnp.sum(all1[:, eighth:].astype(F32), axis=(0, 1))[None]

    head_grad = jnp.zeros((rows, cols), F32)
    for r in range(4):
        piece = after(got_head[r], hid1).astype(F32) * (1.0 / HEAD_SCALE)
        head_grad = lax.dynamic_update_slice(head_grad, piece, (0, (me ^ r) * part))
    token_loss = jnp.concatenate([loss0, loss1]).reshape(batches, tok_count)
    hidden_grad = jnp.concatenate([in_order(all0), in_order(all1[:, :eighth])])
    return token_loss, hidden_grad.reshape(1, batches, tok_count, features), head_grad, gain


def solution(mesh):
    fine = Mesh(mesh.devices.reshape(2, 4, 2, 2, 4), ("s", "y", "h", "c", "t"))
    dp = ("y", "h", "c")
    in_specs = (P("s", None, dp, None), P(None, dp), P(), P(dp, ("s", "t")))
    out_specs = (P(None, dp), P("s", None, dp, None), P(dp, ("s", "t")), P(dp, None))
    return jax.shard_map(local, mesh=fine, in_specs=in_specs, out_specs=out_specs, check_vma=False)
```

```python
import jax
import jax.numpy as jnp
from jax import lax
from jax.sharding import Mesh, PartitionSpec as P

NORM_EPS = 1e-05
CHUNKS = 2
ROW_SCALE = 2.0**17
HEAD_SCALE = 2.0**-3
BF16, F16, F32 = jnp.bfloat16, jnp.float16, jnp.float32


def shift(x, axis, step):
    size = lax.axis_size(axis)
    return lax.ppermute(x, axis, [((i + step) % size, i) for i in range(size)])


def flip(x, axes, bits):
    size = 1
    for axis in axes:
        size *= lax.axis_size(axis)
    return lax.ppermute(x, axes, [(i, i ^ bits) for i in range(size)])


def after(x, y):
    return lax.optimization_barrier((x, y))[0]


def merge(parts):
    top = parts[0][..., 0, :]
    for part in parts[1:]:
        top = jnp.maximum(top, part[..., 0, :])
    totals = [part[..., 1, :] * jnp.exp(part[..., 0, :] - top) for part in parts]
    hits = [part[..., 2, :] for part in parts]
    while len(totals) > 1:
        half = len(totals) // 2
        totals = [totals[i] + totals[i + half] for i in range(half)]
        hits = [hits[i] + hits[i + half] for i in range(half)]
    return jnp.stack([top, totals[0], hits[0]], axis=-2)


def swap(x, axis):
    return lax.all_to_all(x, axis, 0, 0, tiled=True)


def pick(pieces, index):
    return lax.dynamic_index_in_dim(jnp.stack(pieces), index, 0, keepdims=False)


def total(pieces):
    pieces = pieces.astype(F32)
    return (pieces[0] + pieces[2]) + (pieces[1] + pieces[3])


def local(hidden_parts, targets, norm_gain, head_weight):
    s, y, h, c, t = (lax.axis_index(name) for name in ("s", "y", "h", "c", "t"))
    me = 2 * h + c
    rows, cols = head_weight.shape
    part = cols // 4
    width = 4 * rows
    batches, tok_count, features = hidden_parts.shape[1:]
    count = batches * tok_count
    size = count // CHUNKS
    quarter = size // 4
    eighth = quarter // 2

    pieces = [lax.dynamic_slice_in_dim(head_weight, (me ^ r) * part, part, 1) for r in range(4)]
    early = 3 * rows // 4
    arrived = [pieces[0], flip(pieces[1], ("h", "c"), 1)]
    first = flip(pieces[2][:early], ("h", "c"), 2)
    first_column = (me + 4 * (4 * s + t)) * part

    hidden = hidden_parts.reshape(CHUNKS, 4, quarter, features)
    own = lax.dynamic_index_in_dim(hidden, t, 1, keepdims=False).reshape(CHUNKS * quarter, features)
    mixed = own.astype(F32) + flip(own, ("s",), 1).astype(F32)
    radius = jnp.sqrt(jnp.mean(mixed * mixed, axis=-1, keepdims=True) + NORM_EPS)
    unit = mixed / radius
    normed = (norm_gain * unit).astype(BF16)
    over_y = swap(normed.reshape(CHUNKS * quarter, 4, width).transpose(1, 0, 2), "y")
    got = flip(after(over_y, first), ("s", "h"), 3)
    second = flip(after(pieces[2][early:], got), ("h", "c"), 2)
    arrived.append(jnp.concatenate([first, second]))
    arrived.append(flip(after(pieces[3], got), ("h", "c"), 3))
    blocks = jnp.stack(arrived)
    weight = jnp.concatenate([lax.dynamic_index_in_dim(blocks, me ^ a, 0, keepdims=False) for a in range(4)], axis=0)
    over_h = [
        jnp.stack([v.reshape(4, CHUNKS, quarter, width)[:, k] for v in (over_y, got)], axis=1) for k in range(CHUNKS)
    ]
    unit = unit.reshape(CHUNKS, 2, eighth, features)
    radius = radius.reshape(CHUNKS, 2, eighth, 1)

    ids = after(targets.reshape(count), got)
    ids = jnp.stack([ids, flip(ids, ("h",), 1)])
    ids = jnp.stack([ids, flip(ids, ("c",), 1)])

    def gather(k, wait):
        over_t = after(lax.all_gather(over_h[k], "t", axis=0), wait)
        over_c = jnp.stack([over_t, flip(over_t, ("c",), 1)]).transpose(2, 0, 1, 3, 4, 5)
        return lax.optimization_barrier(over_c.reshape(16 * size, width))

    def partial_logits(gathered):
        out = jnp.dot(gathered, weight, preferred_element_type=F32).astype(F16).reshape(4, 4 * size, part)
        return out, swap(out, "y")

    def loss_and_grad(k, pieces, before_last):
        logits = total(pieces)
        here = ids.reshape(2, 2, CHUNKS, 4, quarter)[:, :, k].transpose(0, 2, 1, 3).reshape(-1)
        is_target = lax.broadcasted_iota(jnp.int32, logits.shape, 1) == (here - first_column)[:, None]
        top = jnp.max(logits, axis=1)
        sums = jnp.sum(jnp.exp(logits - top[:, None]), axis=1)
        hit = jnp.sum(jnp.where(is_target, logits, 0.0), axis=1)
        stats = jnp.stack([v.reshape(2, 4, 2, quarter) for v in (top, sums, hit)], axis=3)
        stats = merge([stats, flip(stats, ("c",), 1)[::-1]])
        got = [flip(stats, ("s", "h"), r) for r in range(1, 4)]
        stats = merge([stats, got[0][:, :, ::-1], got[1], got[2][:, :, ::-1]])
        stats = after(stats, before_last)
        stats = merge([stats] + [shift(stats, "t", r) for r in range(1, 4)])
        log_total = stats[..., 0, :] + jnp.log(stats[..., 1, :])
        loss = log_total - stats[..., 2, :]
        grad = (jnp.exp(logits - log_total.reshape(-1)[:, None]) - is_target.astype(F32)).astype(BF16)
        return loss[0, :, 0].reshape(size), grad, lax.all_gather(grad, "y", axis=0, tiled=True)

    def row_product(grads):
        ordered = grads.reshape(4, 2, 4, 2 * quarter, part).transpose(1, 2, 0, 3, 4).reshape(2, 8 * size, part)
        dims = (((1,), (1,)), ((), ()))
        kept, sent = (lax.dot_general(g, weight, dims, preferred_element_type=F32) * ROW_SCALE for g in ordered)
        return kept, sent.astype(F16)

    def head_product(gathered, grads):
        return lax.dot_general(gathered, grads, (((0,), (0,)), ((), ())), preferred_element_type=F32)

    def over_cores(products, wait):
        kept, sent = products
        return (kept + flip(after(sent, wait), ("c",), 1).astype(F32)).astype(F16)

    def over_tensor(kept):
        return swap(kept.reshape(4, 4, 2 * quarter, width), "t")

    def over_z(pieces):
        kept = total(pieces).reshape(4, 2, 2, eighth, width)
        mine = lax.dynamic_index_in_dim(kept, s, 2, keepdims=False)
        other = lax.dynamic_index_in_dim(kept, 1 - s, 2, keepdims=False).astype(F16)
        got = [
            flip(mine[:, 1].astype(F16), ("s", "h"), 1),
            flip(other[:, 0], ("s", "h"), 2),
            flip(other[:, 1], ("s", "h"), 3),
        ]
        return (mine[:, 0] + got[0].astype(F32)) + (got[1].astype(F32) + got[2].astype(F32)), got

    def to_owner(k, summed):
        sent = summed.astype(F16)
        sent = [lax.dynamic_index_in_dim(sent, (y + r) % 4, 0, keepdims=False) for r in range(4)]
        got = [shift(sent[4 - r], "y", r) for r in range(1, 4)]
        blocks = [sent[0]] + got
        row_grads = jnp.concatenate([pick(blocks, (b - y) % 4) for b in range(4)], axis=1).astype(F32) * (1.0 / ROW_SCALE)
        u = lax.dynamic_index_in_dim(unit[k], s, 0, keepdims=False)
        scaled = norm_gain * row_grads
        hidden_grad = scaled - u * jnp.mean(scaled * u, axis=-1, keepdims=True)
        hidden_grad = hidden_grad / lax.dynamic_index_in_dim(radius[k], s, 0, keepdims=False)
        return hidden_grad.astype(BF16), jnp.sum(row_grads * u, axis=0, keepdims=True), got

    def in_order(mine, got):
        return jnp.stack([pick([mine, got], a ^ s) for a in range(2)]).reshape(quarter, features)

    def halves(v):
        upper = v.astype(BF16)
        return [upper, (v - upper.astype(F32)).astype(BF16)]

    def whole(rows):
        return rows[-2:-1].astype(F32) + rows[-1:].astype(F32)

    x0 = gather(0, (arrived[3], ids))
    part0, got0 = partial_logits(x0)
    x1 = gather(1, part0)
    part1, got1 = partial_logits(x1)
    loss0, grad0, grads0 = loss_and_grad(0, got0, got1)
    products0 = row_product(grads0)
    loss1, grad1, grads1 = loss_and_grad(1, after(got1, grad0), products0[1])

    kept0 = over_cores(products0, part1)
    got_t0 = over_tensor(kept0)
    head0 = head_product(x0, after(grads0, grad1))
    summed0, got_z0 = over_z(got_t0)
    hid0, gain0, got_y0 = to_owner(0, summed0)

    grads1 = after(grads1, (head0, kept0))
    products1 = row_product(grads1)
    got_t1 = over_tensor(over_cores(products1, got0))
    head = head0 + head_product(x1, after(grads1, (products1[1], got_t0)))
    head = (head * HEAD_SCALE).astype(F16).reshape(4, rows, part)
    got_head = [lax.dynamic_index_in_dim(head, me ^ r, 0, keepdims=False) for r in range(4)]
    got_head = [got_head[0]] + [flip(after(got_head[r], got_z0), ("h", "c"), r) for r in range(1, 4)]
    summed1, _ = over_z(after(got_t1, got_head[2:]))
    pair0 = flip(after(hid0, (got_head[2:], got_t1)), ("s",), 1)
    whole0 = in_order(hid0, pair0)
    all0 = lax.all_gather(whole0, "t", axis=0, tiled=True)
    hid1, gain1, _ = to_owner(1, after(summed1, pair0))

    sent1 = jnp.concatenate([hid1] + halves(gain0 + gain1), axis=0)
    pair1 = flip(after(sent1, whole0), ("s",), 1)
    whole1 = in_order(hid1, pair1[:eighth])
    whole1 = jnp.concatenate([whole1] + halves(whole(sent1) + whole(pair1)), axis=0)
    all1 = [whole1] + [shift(whole1, "t", r) for r in range(1, 4)]
    gain = (whole(all1[0]) + whole(all1[2])) + (whole(all1[1]) + whole(all1[3]))
    all1 = jnp.concatenate([pick([v[:quarter] for v in all1], (a - t) % 4) for a in range(4)], axis=0)

    head_grad = jnp.zeros((rows, cols), F32)
    for r in range(4):
        piece = after(got_head[r], pair1).astype(F32) * (1.0 / HEAD_SCALE)
        head_grad = lax.dynamic_update_slice(head_grad, piece, (0, (me ^ r) * part))
    token_loss = jnp.concatenate([loss0, loss1]).reshape(batches, tok_count)
    hidden_grad = jnp.concatenate([all0, all1]).astype(F32)
    return token_loss, hidden_grad.reshape(1, batches, tok_count, features), head_grad, gain


def solution(mesh):
    fine = Mesh(mesh.devices.reshape(2, 4, 2, 2, 4), ("s", "y", "h", "c", "t"))
    dp = ("y", "h", "c")
    in_specs = (P("s", None, dp, None), P(None, dp), P(), P(dp, ("s", "t")))
    out_specs = (P(None, dp), P("s", None, dp, None), P(dp, ("s", "t")), P(dp, None))
    return jax.shard_map(local, mesh=fine, in_specs=in_specs, out_specs=out_specs, check_vma=False)
```

```python
import jax
import jax.numpy as jnp
from jax import lax
from jax.sharding import Mesh, PartitionSpec as P

NORM_EPS = 1e-05
CHUNKS = 2
ROW_SCALE = 2.0**17
HEAD_SCALE = 2.0**-3
BF16, F16, F32 = jnp.bfloat16, jnp.float16, jnp.float32


def shift(x, axis, step):
    size = lax.axis_size(axis)
    return lax.ppermute(x, axis, [((i + step) % size, i) for i in range(size)])


def flip(x, axes, bits):
    size = 1
    for axis in axes:
        size *= lax.axis_size(axis)
    return lax.ppermute(x, axes, [(i, i ^ bits) for i in range(size)])


def after(x, y):
    return lax.optimization_barrier((x, y))[0]


def merge(parts):
    top = parts[0][..., 0, :]
    for part in parts[1:]:
        top = jnp.maximum(top, part[..., 0, :])
    totals = [part[..., 1, :] * jnp.exp(part[..., 0, :] - top) for part in parts]
    hits = [part[..., 2, :] for part in parts]
    while len(totals) > 1:
        half = len(totals) // 2
        totals = [totals[i] + totals[i + half] for i in range(half)]
        hits = [hits[i] + hits[i + half] for i in range(half)]
    return jnp.stack([top, totals[0], hits[0]], axis=-2)


def swap(x, axis):
    return lax.all_to_all(x, axis, 0, 0, tiled=True)


def spread(x, axis):
    return swap(jnp.broadcast_to(x[None], (lax.axis_size(axis),) + x.shape), axis)


def pick(pieces, index):
    return lax.dynamic_index_in_dim(jnp.stack(pieces), index, 0, keepdims=False)


def total(pieces):
    pieces = [pieces[i].astype(F32) for i in range(4)]
    return (pieces[0] + pieces[2]) + (pieces[1] + pieces[3])


def local(hidden_parts, targets, norm_gain, head_weight):
    s, y, h, c, t = (lax.axis_index(name) for name in ("s", "y", "h", "c", "t"))
    me = 2 * h + c
    rows, cols = head_weight.shape
    part = cols // 4
    width = 4 * rows
    batches, tok_count, features = hidden_parts.shape[1:]
    count = batches * tok_count
    size = count // CHUNKS
    quarter = size // 4
    eighth = quarter // 2

    pieces = [lax.dynamic_slice_in_dim(head_weight, (me ^ r) * part, part, 1) for r in range(4)]
    early = 3 * rows // 4
    arrived = [pieces[0], flip(pieces[1], ("h", "c"), 1)]
    first = flip(pieces[2][:early], ("h", "c"), 2)
    first_column = (me + 4 * (4 * s + t)) * part

    hidden = hidden_parts.reshape(CHUNKS, 4, quarter, features)
    own = lax.dynamic_index_in_dim(hidden, t, 1, keepdims=False).reshape(CHUNKS * quarter, features)
    mixed = own.astype(F32) + flip(own, ("s",), 1).astype(F32)
    radius = jnp.sqrt(jnp.mean(mixed * mixed, axis=-1, keepdims=True) + NORM_EPS)
    unit = mixed / radius
    normed = (norm_gain * unit).astype(BF16)
    over_y = swap(normed.reshape(CHUNKS * quarter, 4, width).transpose(1, 0, 2), "y")
    got = flip(after(over_y, first), ("s", "h"), 3)
    second = flip(after(pieces[2][early:], got), ("h", "c"), 2)
    arrived.append(jnp.concatenate([first, second]))
    arrived.append(flip(after(pieces[3], second), ("h", "c"), 3))
    blocks = jnp.stack(arrived)
    weight = jnp.concatenate([lax.dynamic_index_in_dim(blocks, me ^ a, 0, keepdims=False) for a in range(4)], axis=0)
    over_h = [
        jnp.stack([v.reshape(4, CHUNKS, quarter, width)[:, k] for v in (over_y, got)], axis=1) for k in range(CHUNKS)
    ]
    unit = unit.reshape(CHUNKS, 2, eighth, features)
    radius = radius.reshape(CHUNKS, 2, eighth, 1)

    ids = after(targets.reshape(count), got)
    ids = jnp.stack([ids, flip(ids, ("h",), 1)])
    ids = jnp.stack([ids, flip(ids, ("c",), 1)])

    def gather(over_t):
        over_c = jnp.stack([over_t, flip(over_t, ("c",), 1)]).transpose(2, 0, 1, 3, 4, 5)
        return lax.optimization_barrier(over_c.reshape(16 * size, width))

    def partial_logits(gathered):
        out = jnp.dot(gathered, weight, preferred_element_type=F32).astype(F16).reshape(4, 4 * size, part)
        return out, swap(out, "y")

    def loss_and_grad(k, pieces, before_last):
        logits = total(pieces)
        here = ids.reshape(2, 2, CHUNKS, 4, quarter)[:, :, k].transpose(0, 2, 1, 3).reshape(-1)
        is_target = lax.broadcasted_iota(jnp.int32, logits.shape, 1) == (here - first_column)[:, None]
        top = jnp.max(logits, axis=1)
        sums = jnp.sum(jnp.exp(logits - top[:, None]), axis=1)
        hit = jnp.sum(jnp.where(is_target, logits, 0.0), axis=1)
        stats = jnp.stack([v.reshape(2, 4, 2, quarter) for v in (top, sums, hit)], axis=3)
        stats = merge([stats, flip(stats, ("c",), 1)[::-1]])
        got = [flip(stats, ("s", "h"), r) for r in range(1, 4)]
        stats = merge([stats, got[0][:, :, ::-1], got[1], got[2][:, :, ::-1]])
        if before_last is not None:
            stats = after(stats, before_last)
        stats = merge([stats] + [shift(stats, "t", r) for r in range(1, 4)])
        log_total = stats[..., 0, :] + jnp.log(stats[..., 1, :])
        loss = log_total - stats[..., 2, :]
        grad = (jnp.exp(logits - log_total.reshape(-1)[:, None]) - is_target.astype(F32)).astype(BF16)
        return loss[0, :, 0].reshape(size), grad

    def row_product(grads):
        ordered = grads.reshape(4, 2, 4, 2 * quarter, part).transpose(1, 2, 0, 3, 4).reshape(2, 8 * size, part)
        dims = (((1,), (1,)), ((), ()))
        kept, sent = (lax.dot_general(g, weight, dims, preferred_element_type=F32) * ROW_SCALE for g in ordered)
        return lax.optimization_barrier(kept), sent.astype(F16)

    def head_product(gathered, grads):
        return lax.dot_general(gathered, grads, (((0,), (0,)), ((), ())), preferred_element_type=F32)

    def over_cores(products):
        kept, sent = products
        kept = (kept + flip(sent, ("c",), 1).astype(F32)).astype(F16)
        return kept.reshape(4, 4, 2 * quarter, width)

    def to_places(pieces, index, axis):
        sent = [lax.dynamic_index_in_dim(pieces, (index + r) % 4, 0, keepdims=False) for r in range(4)]
        return [sent[0]] + [shift(sent[4 - r], axis, r) for r in range(1, 4)]

    def over_z(pieces):
        kept = total(pieces).reshape(4, 2, 2, eighth, width)
        mine = lax.dynamic_index_in_dim(kept, s, 2, keepdims=False)
        other = lax.dynamic_index_in_dim(kept, 1 - s, 2, keepdims=False).astype(F16)
        got = [
            flip(mine[:, 1].astype(F16), ("s", "h"), 1),
            flip(other[:, 0], ("s", "h"), 2),
            flip(other[:, 1], ("s", "h"), 3),
        ]
        return (mine[:, 0] + got[0].astype(F32)) + (got[1].astype(F32) + got[2].astype(F32)), got

    def to_owner(k, summed):
        blocks = to_places(summed.astype(F16), y, "y")
        row_grads = jnp.concatenate([pick(blocks, (b - y) % 4) for b in range(4)], axis=1).astype(F32) * (1.0 / ROW_SCALE)
        u = lax.dynamic_index_in_dim(unit[k], s, 0, keepdims=False)
        scaled = norm_gain * row_grads
        hidden_grad = scaled - u * jnp.mean(scaled * u, axis=-1, keepdims=True)
        hidden_grad = hidden_grad / lax.dynamic_index_in_dim(radius[k], s, 0, keepdims=False)
        return hidden_grad.astype(BF16), jnp.sum(row_grads * u, axis=0, keepdims=True)

    def in_order(mine, got):
        return jnp.stack([pick([mine, got], a ^ s) for a in range(2)]).reshape(quarter, features)

    def halves(v):
        upper = v.astype(BF16)
        return [upper, (v - upper.astype(F32)).astype(BF16)]

    def whole(rows):
        return rows[-2:-1].astype(F32) + rows[-1:].astype(F32)

    x0 = gather(after(spread(over_h[0], "t"), (arrived[3], ids)))
    part0, got0 = partial_logits(x0)
    pieces = after([shift(over_h[1], "t", r) for r in range(1, 4)], part0)
    x1 = gather(jnp.stack([pick([over_h[1]] + pieces, (a - t) % 4) for a in range(4)]))
    part1, got1 = partial_logits(x1)
    loss0, grad0 = loss_and_grad(0, after(got0, part1), got1)
    grads0 = spread(grad0, "y").reshape(16 * size, part)
    loss1, grad1 = loss_and_grad(1, after(got1, grad0), None)
    grads1 = [grad1] + [shift(grad1, "y", r) for r in range(1, 4)]

    kept0 = over_cores(row_product(grads0))
    got_t0 = swap(kept0, "t")
    head0 = head_product(x0, after(grads0, (grad1, kept0)))
    summed0, got_z0 = over_z(got_t0)
    hid0, gain0 = to_owner(0, summed0)

    grads1 = after(grads1, (head0, kept0))
    grads1 = jnp.concatenate([pick(grads1, (a - y) % 4) for a in range(4)], axis=0)
    grads1 = lax.optimization_barrier(grads1)
    products1 = row_product(grads1)
    got_t1 = swap(over_cores(products1), "t")
    head = head0 + head_product(x1, after(grads1, (products1[1], got_z0)))
    head = (head * HEAD_SCALE).astype(F16).reshape(4, rows, part)
    got_head = [lax.dynamic_index_in_dim(head, me ^ r, 0, keepdims=False) for r in range(4)]
    got_head[1] = flip(after(got_head[1], got_z0), ("h", "c"), 1)
    got_head[2] = flip(after(got_head[2], got_z0), ("h", "c"), 2)
    summed1, got_z1 = over_z(after(got_t1, got_head[2]))
    pair0 = flip(after(hid0, (got_head[2], got_t1)), ("s",), 1)
    got_head[3] = flip(after(got_head[3], (got_z1, pair0)), ("h", "c"), 3)
    all0 = spread(in_order(hid0, pair0), "t").reshape(size, features)
    hid1, gain1 = to_owner(1, after(summed1, pair0))

    sent1 = jnp.concatenate([hid1] + halves(gain0 + gain1), axis=0)
    pair1 = flip(after(sent1, (all0, got_head[3])), ("s",), 1)
    whole1 = in_order(hid1, pair1[:eighth])
    whole1 = jnp.concatenate([whole1] + halves(whole(sent1) + whole(pair1)), axis=0)
    all1 = [whole1] + [shift(whole1, "t", r) for r in range(1, 4)]
    gain = (whole(all1[0]) + whole(all1[2])) + (whole(all1[1]) + whole(all1[3]))
    all1 = jnp.concatenate([pick([v[:quarter] for v in all1], (a - t) % 4) for a in range(4)], axis=0)

    head_grad = jnp.zeros((rows, cols), F32)
    for r in range(4):
        piece = after(got_head[r], pair1).astype(F32) * (1.0 / HEAD_SCALE)
        head_grad = lax.dynamic_update_slice(head_grad, piece, (0, (me ^ r) * part))
    token_loss = jnp.concatenate([loss0, loss1]).reshape(batches, tok_count)
    hidden_grad = jnp.concatenate([all0, all1]).astype(F32)
    return token_loss, hidden_grad.reshape(1, batches, tok_count, features), head_grad, gain


def solution(mesh):
    fine = Mesh(mesh.devices.reshape(2, 4, 2, 2, 4), ("s", "y", "h", "c", "t"))
    dp = ("y", "h", "c")
    in_specs = (P("s", None, dp, None), P(None, dp), P(), P(dp, ("s", "t")))
    out_specs = (P(None, dp), P("s", None, dp, None), P(dp, ("s", "t")), P(dp, None))
    return jax.shard_map(local, mesh=fine, in_specs=in_specs, out_specs=out_specs, check_vma=False)
```

```python
import jax
import jax.numpy as jnp
from jax import lax
from jax.sharding import Mesh, PartitionSpec as P

NORM_EPS = 1e-05
CHUNKS = 2
ROW_SCALE = 2.0**17
HEAD_SCALE = 2.0**-3
BF16, F16, F32 = jnp.bfloat16, jnp.float16, jnp.float32


def shift(x, axis, step):
    size = lax.axis_size(axis)
    return lax.ppermute(x, axis, [((i + step) % size, i) for i in range(size)])


def flip(x, axes, bits):
    size = 1
    for axis in axes:
        size *= lax.axis_size(axis)
    return lax.ppermute(x, axes, [(i, i ^ bits) for i in range(size)])


def after(x, y):
    return lax.optimization_barrier((x, y))[0]


def merge(parts):
    top = parts[0][..., 0, :]
    for part in parts[1:]:
        top = jnp.maximum(top, part[..., 0, :])
    totals = [part[..., 1, :] * jnp.exp(part[..., 0, :] - top) for part in parts]
    hits = [part[..., 2, :] for part in parts]
    while len(totals) > 1:
        half = len(totals) // 2
        totals = [totals[i] + totals[i + half] for i in range(half)]
        hits = [hits[i] + hits[i + half] for i in range(half)]
    return jnp.stack([top, totals[0], hits[0]], axis=-2)


def swap(x, axis):
    return lax.all_to_all(x, axis, 0, 0, tiled=True)


def spread(x, axis):
    return swap(jnp.broadcast_to(x[None], (lax.axis_size(axis),) + x.shape), axis)


def pick(pieces, index):
    return lax.dynamic_index_in_dim(jnp.stack(pieces), index, 0, keepdims=False)


def total(pieces):
    pieces = [pieces[i].astype(F32) for i in range(4)]
    return (pieces[0] + pieces[2]) + (pieces[1] + pieces[3])


def local(hidden_parts, targets, norm_gain, head_weight):
    s, y, h, c, t = (lax.axis_index(name) for name in ("s", "y", "h", "c", "t"))
    me = 2 * h + c
    rows, cols = head_weight.shape
    part = cols // 4
    width = 4 * rows
    batches, tok_count, features = hidden_parts.shape[1:]
    count = batches * tok_count
    size = count // CHUNKS
    quarter = size // 4
    eighth = quarter // 2

    pieces = [lax.dynamic_slice_in_dim(head_weight, (me ^ r) * part, part, 1) for r in range(4)]
    early = 3 * rows // 4
    arrived = [pieces[0], flip(pieces[1], ("h", "c"), 1)]
    first = flip(pieces[2][:early], ("h", "c"), 2)
    first_column = (me + 4 * (4 * s + t)) * part

    hidden = hidden_parts.reshape(CHUNKS, 4, quarter, features)
    own = lax.dynamic_index_in_dim(hidden, t, 1, keepdims=False).reshape(CHUNKS * quarter, features)
    mixed = own.astype(F32) + flip(own, ("s",), 1).astype(F32)
    radius = jnp.sqrt(jnp.mean(mixed * mixed, axis=-1, keepdims=True) + NORM_EPS)
    unit = mixed / radius
    normed = (norm_gain * unit).astype(BF16)
    over_y = swap(normed.reshape(CHUNKS * quarter, 4, width).transpose(1, 0, 2), "y")
    got = flip(after(over_y, first), ("s", "h"), 3)
    second = flip(after(pieces[2][early:], got), ("h", "c"), 2)
    arrived.append(jnp.concatenate([first, second]))
    arrived.append(flip(after(pieces[3], second), ("h", "c"), 3))
    blocks = jnp.stack(arrived)
    weight = jnp.concatenate([lax.dynamic_index_in_dim(blocks, me ^ a, 0, keepdims=False) for a in range(4)], axis=0)
    over_h = [
        jnp.stack([v.reshape(4, CHUNKS, quarter, width)[:, k] for v in (over_y, got)], axis=1) for k in range(CHUNKS)
    ]
    unit = unit.reshape(CHUNKS, 2, eighth, features)
    radius = radius.reshape(CHUNKS, 2, eighth, 1)

    ids = after(targets.reshape(count), got)
    ids = jnp.stack([ids, flip(ids, ("h",), 1)])
    ids = jnp.stack([ids, flip(ids, ("c",), 1)])

    def gather(over_t):
        over_c = jnp.stack([over_t, flip(over_t, ("c",), 1)]).transpose(2, 0, 1, 3, 4, 5)
        return lax.optimization_barrier(over_c.reshape(16 * size, width))

    def partial_logits(gathered):
        out = jnp.dot(gathered, weight, preferred_element_type=F32).astype(F16).reshape(4, 4 * size, part)
        return out, swap(out, "y")

    def loss_and_grad(k, pieces, before_last):
        logits = total(pieces)
        here = ids.reshape(2, 2, CHUNKS, 4, quarter)[:, :, k].transpose(0, 2, 1, 3).reshape(-1)
        is_target = lax.broadcasted_iota(jnp.int32, logits.shape, 1) == (here - first_column)[:, None]
        top = jnp.max(logits, axis=1)
        sums = jnp.sum(jnp.exp(logits - top[:, None]), axis=1)
        hit = jnp.sum(jnp.where(is_target, logits, 0.0), axis=1)
        stats = jnp.stack([v.reshape(2, 4, 2, quarter) for v in (top, sums, hit)], axis=3)
        stats = merge([stats, flip(stats, ("c",), 1)[::-1]])
        got = [flip(stats, ("s", "h"), r) for r in range(1, 4)]
        stats = merge([stats, got[0][:, :, ::-1], got[1], got[2][:, :, ::-1]])
        if before_last is not None:
            stats = after(stats, before_last)
        stats = merge([stats] + [shift(stats, "t", r) for r in range(1, 4)])
        log_total = stats[..., 0, :] + jnp.log(stats[..., 1, :])
        loss = log_total - stats[..., 2, :]
        grad = (jnp.exp(logits - log_total.reshape(-1)[:, None]) - is_target.astype(F32)).astype(BF16)
        return loss[0, :, 0].reshape(size), grad

    def row_product(grads):
        ordered = grads.reshape(4, 2, 4, 2 * quarter, part).transpose(1, 2, 0, 3, 4).reshape(16 * size, part)
        product = lax.dot_general(ordered, weight, (((1,), (1,)), ((), ())), preferred_element_type=F32)
        return lax.optimization_barrier((product * ROW_SCALE).astype(F16).reshape(2, 8 * size, width))

    def head_product(gathered, grads):
        return lax.dot_general(gathered, grads, (((0,), (0,)), ((), ())), preferred_element_type=F32)

    def over_cores(products):
        kept, sent = products
        kept = (kept.astype(F32) + flip(sent, ("c",), 1).astype(F32)).astype(F16)
        return kept.reshape(4, 4, 2 * quarter, width)

    def to_places(pieces, index, axis):
        sent = [lax.dynamic_index_in_dim(pieces, (index + r) % 4, 0, keepdims=False) for r in range(4)]
        return [sent[0]] + [shift(sent[4 - r], axis, r) for r in range(1, 4)]

    def over_z(pieces):
        kept = total(pieces).reshape(4, 2, 2, eighth, width)
        mine = lax.dynamic_index_in_dim(kept, s, 2, keepdims=False)
        other = lax.dynamic_index_in_dim(kept, 1 - s, 2, keepdims=False).astype(F16)
        got = [
            flip(mine[:, 1].astype(F16), ("s", "h"), 1),
            flip(other[:, 0], ("s", "h"), 2),
            flip(other[:, 1], ("s", "h"), 3),
        ]
        return (mine[:, 0] + got[0].astype(F32)) + (got[1].astype(F32) + got[2].astype(F32)), got

    def to_owner(k, summed):
        blocks = to_places(summed.astype(F16), y, "y")
        row_grads = jnp.concatenate([pick(blocks, (b - y) % 4) for b in range(4)], axis=1).astype(F32) * (1.0 / ROW_SCALE)
        u = lax.dynamic_index_in_dim(unit[k], s, 0, keepdims=False)
        scaled = norm_gain * row_grads
        hidden_grad = scaled - u * jnp.mean(scaled * u, axis=-1, keepdims=True)
        hidden_grad = hidden_grad / lax.dynamic_index_in_dim(radius[k], s, 0, keepdims=False)
        return hidden_grad.astype(BF16), jnp.sum(row_grads * u, axis=0, keepdims=True)

    def in_order(mine, got):
        return jnp.stack([pick([mine, got], a ^ s) for a in range(2)]).reshape(quarter, features)

    def halves(v):
        upper = v.astype(BF16)
        return [upper, (v - upper.astype(F32)).astype(BF16)]

    def whole(rows):
        return rows[-2:-1].astype(F32) + rows[-1:].astype(F32)

    x0 = gather(after(spread(over_h[0], "t"), (arrived[3], ids)))
    part0, got0 = partial_logits(x0)
    pieces = after([shift(over_h[1], "t", r) for r in range(1, 4)], got0)
    x1 = gather(jnp.stack([pick([over_h[1]] + pieces, (a - t) % 4) for a in range(4)]))
    part1, got1 = partial_logits(x1)
    loss0, grad0 = loss_and_grad(0, got0, part1)
    grads0 = spread(after(grad0, got1), "y").reshape(16 * size, part)
    loss1, grad1 = loss_and_grad(1, after(got1, grad0), None)
    grads1 = [grad1] + [shift(grad1, "y", r) for r in range(1, 4)]

    kept0 = over_cores(row_product(grads0))
    got_t0 = swap(kept0, "t")
    head0 = head_product(x0, after(grads0, (grad1, kept0)))
    summed0, got_z0 = over_z(got_t0)
    hid0, gain0 = to_owner(0, summed0)

    grads1 = after(grads1, (head0, kept0))
    grads1 = jnp.concatenate([pick(grads1, (a - y) % 4) for a in range(4)], axis=0)
    grads1 = lax.optimization_barrier(grads1)
    products1 = row_product(grads1)
    got_t1 = swap(over_cores(products1), "t")
    head = head0 + head_product(x1, after(grads1, (products1, got_z0)))
    head = (head * HEAD_SCALE).astype(F16).reshape(4, rows, part)
    got_head = [lax.dynamic_index_in_dim(head, me ^ r, 0, keepdims=False) for r in range(4)]
    got_head = [got_head[0]] + [flip(after(got_head[r], got_z0), ("h", "c"), r) for r in range(1, 4)]
    summed1, _ = over_z(after(got_t1, got_head[2:]))
    pair0 = flip(after(hid0, (got_head[2:], got_t1)), ("s",), 1)
    all0 = spread(in_order(hid0, pair0), "t").reshape(size, features)
    hid1, gain1 = to_owner(1, after(summed1, pair0))

    sent1 = jnp.concatenate([hid1] + halves(gain0 + gain1), axis=0)
    pair1 = flip(after(sent1, all0), ("s",), 1)
    whole1 = in_order(hid1, pair1[:eighth])
    whole1 = jnp.concatenate([whole1] + halves(whole(sent1) + whole(pair1)), axis=0)
    all1 = [whole1] + [shift(whole1, "t", r) for r in range(1, 4)]
    gain = (whole(all1[0]) + whole(all1[2])) + (whole(all1[1]) + whole(all1[3]))
    all1 = jnp.concatenate([pick([v[:quarter] for v in all1], (a - t) % 4) for a in range(4)], axis=0)

    head_grad = jnp.zeros((rows, cols), F32)
    for r in range(4):
        piece = after(got_head[r], pair1).astype(F32) * (1.0 / HEAD_SCALE)
        head_grad = lax.dynamic_update_slice(head_grad, piece, (0, (me ^ r) * part))
    token_loss = jnp.concatenate([loss0, loss1]).reshape(batches, tok_count)
    hidden_grad = jnp.concatenate([all0, all1]).astype(F32)
    return token_loss, hidden_grad.reshape(1, batches, tok_count, features), head_grad, gain


def solution(mesh):
    fine = Mesh(mesh.devices.reshape(2, 4, 2, 2, 4), ("s", "y", "h", "c", "t"))
    dp = ("y", "h", "c")
    in_specs = (P("s", None, dp, None), P(None, dp), P(), P(dp, ("s", "t")))
    out_specs = (P(None, dp), P("s", None, dp, None), P(dp, ("s", "t")), P(dp, None))
    return jax.shard_map(local, mesh=fine, in_specs=in_specs, out_specs=out_specs, check_vma=False)
```

```python
import jax
import jax.numpy as jnp
from jax import lax
from jax.sharding import Mesh, PartitionSpec as P

NORM_EPS = 1e-05
CHUNKS = 2
ROW_SCALE = 2.0**17
HEAD_SCALE = 2.0**-3
BF16, F16, F32 = jnp.bfloat16, jnp.float16, jnp.float32


def shift(x, axis, step):
    size = lax.axis_size(axis)
    return lax.ppermute(x, axis, [((i + step) % size, i) for i in range(size)])


def flip(x, axes, bits):
    size = 1
    for axis in axes:
        size *= lax.axis_size(axis)
    return lax.ppermute(x, axes, [(i, i ^ bits) for i in range(size)])


def after(x, y):
    return lax.optimization_barrier((x, y))[0]


def merge(parts):
    top = parts[0][..., 0, :]
    for part in parts[1:]:
        top = jnp.maximum(top, part[..., 0, :])
    totals = [part[..., 1, :] * jnp.exp(part[..., 0, :] - top) for part in parts]
    hits = [part[..., 2, :] for part in parts]
    while len(totals) > 1:
        half = len(totals) // 2
        totals = [totals[i] + totals[i + half] for i in range(half)]
        hits = [hits[i] + hits[i + half] for i in range(half)]
    return jnp.stack([top, totals[0], hits[0]], axis=-2)


def swap(x, axis):
    return lax.all_to_all(x, axis, 0, 0, tiled=True)


def spread(x, axis):
    return swap(jnp.broadcast_to(x[None], (lax.axis_size(axis),) + x.shape), axis)


def pick(pieces, index):
    return lax.dynamic_index_in_dim(jnp.stack(pieces), index, 0, keepdims=False)


def total(pieces):
    pieces = [pieces[i].astype(F32) for i in range(4)]
    return (pieces[0] + pieces[2]) + (pieces[1] + pieces[3])


def local(hidden_parts, targets, norm_gain, head_weight):
    s, y, h, c, t = (lax.axis_index(name) for name in ("s", "y", "h", "c", "t"))
    me = 2 * h + c
    rows, cols = head_weight.shape
    part = cols // 4
    width = 4 * rows
    batches, tok_count, features = hidden_parts.shape[1:]
    count = batches * tok_count
    size = count // CHUNKS
    quarter = size // 4
    eighth = quarter // 2

    pieces = [lax.dynamic_slice_in_dim(head_weight, (me ^ r) * part, part, 1) for r in range(4)]
    early = 3 * rows // 4
    arrived = [pieces[0], flip(pieces[1], ("h", "c"), 1)]
    first = flip(pieces[2][:early], ("h", "c"), 2)
    first_column = (me + 4 * (4 * s + t)) * part

    hidden = hidden_parts.reshape(CHUNKS, 4, quarter, features)
    own = lax.dynamic_index_in_dim(hidden, t, 1, keepdims=False).reshape(CHUNKS * quarter, features)
    mixed = own.astype(F32) + flip(own, ("s",), 1).astype(F32)
    radius = jnp.sqrt(jnp.mean(mixed * mixed, axis=-1, keepdims=True) + NORM_EPS)
    unit = mixed / radius
    normed = (norm_gain * unit).astype(BF16)
    over_y = swap(normed.reshape(CHUNKS * quarter, 4, width).transpose(1, 0, 2), "y")
    got = flip(after(over_y, first), ("s", "h"), 3)
    second = flip(after(pieces[2][early:], got), ("h", "c"), 2)
    arrived.append(jnp.concatenate([first, second]))
    arrived.append(flip(after(pieces[3], second), ("h", "c"), 3))
    blocks = jnp.stack(arrived)
    weight = jnp.concatenate([lax.dynamic_index_in_dim(blocks, me ^ a, 0, keepdims=False) for a in range(4)], axis=0)
    over_h = jnp.stack([v.reshape(4, CHUNKS, quarter, width).transpose(1, 0, 2, 3) for v in (over_y, got)], axis=2)
    over_t = spread(over_h, "t")
    unit = unit.reshape(CHUNKS, 2, eighth, features)
    radius = radius.reshape(CHUNKS, 2, eighth, 1)

    ids = after(targets.reshape(count), got)
    ids = jnp.stack([ids, flip(ids, ("h",), 1)])
    ids = jnp.stack([ids, flip(ids, ("c",), 1)])

    def gather(over_t):
        over_c = jnp.stack([over_t, flip(over_t, ("c",), 1)]).transpose(2, 0, 1, 3, 4, 5)
        return lax.optimization_barrier(over_c.reshape(16 * size, width))

    def partial_logits(gathered):
        out = jnp.dot(gathered, weight, preferred_element_type=F32).astype(F16).reshape(4, 4 * size, part)
        return out, swap(out, "y")

    def statistics(k, pieces):
        logits = total(pieces)
        here = ids.reshape(2, 2, CHUNKS, 4, quarter)[:, :, k].transpose(0, 2, 1, 3).reshape(-1)
        is_target = lax.broadcasted_iota(jnp.int32, logits.shape, 1) == (here - first_column)[:, None]
        top = jnp.max(logits, axis=1)
        sums = jnp.sum(jnp.exp(logits - top[:, None]), axis=1)
        hit = jnp.sum(jnp.where(is_target, logits, 0.0), axis=1)
        stats = jnp.stack([v.reshape(2, 4, 2, quarter) for v in (top, sums, hit)], axis=3)
        stats = merge([stats, flip(stats, ("c",), 1)[::-1]])
        got = [flip(stats, ("s", "h"), r) for r in range(1, 4)]
        stats = merge([stats, got[0][:, :, ::-1], got[1], got[2][:, :, ::-1]])
        return logits, is_target, stats

    def loss_and_grad(logits, is_target, stats):
        stats = merge([stats] + [shift(stats, "t", r) for r in range(1, 4)])
        log_total = stats[..., 0, :] + jnp.log(stats[..., 1, :])
        loss = log_total - stats[..., 2, :]
        grad = (jnp.exp(logits - log_total.reshape(-1)[:, None]) - is_target.astype(F32)).astype(BF16)
        return loss[0, :, 0].reshape(size), grad

    def row_product(grads):
        ordered = grads.reshape(4, 2, 4, 2 * quarter, part).transpose(1, 2, 0, 3, 4).reshape(16 * size, part)
        product = lax.dot_general(ordered, weight, (((1,), (1,)), ((), ())), preferred_element_type=F32)
        return lax.optimization_barrier((product * ROW_SCALE).astype(F16).reshape(2, 8 * size, width))

    def head_product(gathered, grads):
        return lax.dot_general(gathered, grads, (((0,), (0,)), ((), ())), preferred_element_type=F32)

    def over_cores(products):
        kept, sent = products
        kept = (kept.astype(F32) + flip(sent, ("c",), 1).astype(F32)).astype(F16)
        return kept.reshape(4, 4, 2 * quarter, width)

    def to_places(pieces, index, axis):
        sent = [lax.dynamic_index_in_dim(pieces, (index + r) % 4, 0, keepdims=False) for r in range(4)]
        return [sent[0]] + [shift(sent[4 - r], axis, r) for r in range(1, 4)]

    def over_z(pieces):
        kept = total(pieces).reshape(4, 2, 2, eighth, width)
        mine = lax.dynamic_index_in_dim(kept, s, 2, keepdims=False)
        other = lax.dynamic_index_in_dim(kept, 1 - s, 2, keepdims=False).astype(F16)
        got = [
            flip(mine[:, 1].astype(F16), ("s", "h"), 1),
            flip(other[:, 0], ("s", "h"), 2),
            flip(other[:, 1], ("s", "h"), 3),
        ]
        return (mine[:, 0] + got[0].astype(F32)) + (got[1].astype(F32) + got[2].astype(F32)), got

    def to_owner(k, summed):
        blocks = to_places(summed.astype(F16), y, "y")
        row_grads = jnp.concatenate([pick(blocks, (b - y) % 4) for b in range(4)], axis=1).astype(F32) * (1.0 / ROW_SCALE)
        u = lax.dynamic_index_in_dim(unit[k], s, 0, keepdims=False)
        scaled = norm_gain * row_grads
        hidden_grad = scaled - u * jnp.mean(scaled * u, axis=-1, keepdims=True)
        hidden_grad = hidden_grad / lax.dynamic_index_in_dim(radius[k], s, 0, keepdims=False)
        return hidden_grad.astype(BF16), jnp.sum(row_grads * u, axis=0, keepdims=True)

    def in_order(mine, got):
        return jnp.stack([pick([mine, got], a ^ s) for a in range(2)]).reshape(quarter, features)

    def halves(v):
        upper = v.astype(BF16)
        return [upper, (v - upper.astype(F32)).astype(BF16)]

    def whole(rows):
        return rows[-2:-1].astype(F32) + rows[-1:].astype(F32)

    first_rows, ids = lax.optimization_barrier((over_t[:, 0], ids))
    x0 = gather(after(first_rows, arrived[3]))
    part0, got0 = partial_logits(x0)
    x1 = gather(over_t[:, 1])
    part1, got1 = partial_logits(x1)
    logits0, hits0, stats0 = statistics(0, after(got0, part1))
    got1, stats0 = lax.optimization_barrier((got1, stats0))
    loss0, grad0 = loss_and_grad(logits0, hits0, stats0)
    got1, grad0 = lax.optimization_barrier((got1, grad0))
    grads0 = spread(grad0, "y").reshape(16 * size, part)
    loss1, grad1 = loss_and_grad(*statistics(1, got1))
    grads1 = [grad1] + [shift(grad1, "y", r) for r in range(1, 4)]

    kept0 = over_cores(row_product(after(grads0, grad1)))
    got_t0 = swap(kept0, "t")
    head0 = head_product(x0, after(grads0, (grad1, kept0)))
    summed0, got_z0 = over_z(got_t0)
    hid0, gain0 = to_owner(0, summed0)

    grads1 = after(grads1, (head0, kept0))
    grads1 = jnp.concatenate([pick(grads1, (a - y) % 4) for a in range(4)], axis=0)
    grads1 = lax.optimization_barrier(grads1)
    products1 = row_product(grads1)
    got_t1 = swap(over_cores(products1), "t")
    head = head0 + head_product(x1, after(grads1, (products1, got_z0)))
    head = (head * HEAD_SCALE).astype(F16).reshape(4, rows, part)
    got_head = [lax.dynamic_index_in_dim(head, me ^ r, 0, keepdims=False) for r in range(4)]
    got_head = [got_head[0]] + [flip(after(got_head[r], got_z0), ("h", "c"), r) for r in range(1, 4)]
    summed1, _ = over_z(after(got_t1, got_head[2:]))
    pair0 = flip(after(hid0, (got_head[2:], got_t1)), ("s",), 1)
    all0 = spread(in_order(hid0, pair0), "t").reshape(size, features)
    hid1, gain1 = to_owner(1, after(summed1, pair0))

    sent1 = jnp.concatenate([hid1] + halves(gain0 + gain1), axis=0)
    pair1 = flip(after(sent1, pair0), ("s",), 1)
    whole1 = in_order(hid1, pair1[:eighth])
    whole1 = jnp.concatenate([whole1] + halves(whole(sent1) + whole(pair1)), axis=0)
    all1 = [whole1] + [shift(whole1, "t", r) for r in range(1, 4)]
    gain = (whole(all1[0]) + whole(all1[2])) + (whole(all1[1]) + whole(all1[3]))
    all1 = jnp.concatenate([pick([v[:quarter] for v in all1], (a - t) % 4) for a in range(4)], axis=0)

    head_grad = jnp.zeros((rows, cols), F32)
    for r in range(4):
        piece = after(got_head[r], pair1).astype(F32) * (1.0 / HEAD_SCALE)
        head_grad = lax.dynamic_update_slice(head_grad, piece, (0, (me ^ r) * part))
    token_loss = jnp.concatenate([loss0, loss1]).reshape(batches, tok_count)
    hidden_grad = jnp.concatenate([all0, all1]).astype(F32)
    return token_loss, hidden_grad.reshape(1, batches, tok_count, features), head_grad, gain


def solution(mesh):
    fine = Mesh(mesh.devices.reshape(2, 4, 2, 2, 4), ("s", "y", "h", "c", "t"))
    dp = ("y", "h", "c")
    in_specs = (P("s", None, dp, None), P(None, dp), P(), P(dp, ("s", "t")))
    out_specs = (P(None, dp), P("s", None, dp, None), P(dp, ("s", "t")), P(dp, None))
    return jax.shard_map(local, mesh=fine, in_specs=in_specs, out_specs=out_specs, check_vma=False)
```

```python
import jax
import jax.numpy as jnp
from jax import lax
from jax.sharding import Mesh, PartitionSpec as P

NORM_EPS = 1e-05
CHUNKS = 1
ROW_SCALE = 2.0**17
HEAD_SCALE = 2.0**-3
BF16, F16, F32 = jnp.bfloat16, jnp.float16, jnp.float32


def shift(x, axis, step):
    size = lax.axis_size(axis)
    return lax.ppermute(x, axis, [((i + step) % size, i) for i in range(size)])


def flip(x, axes, bits):
    size = 1
    for axis in axes:
        size *= lax.axis_size(axis)
    return lax.ppermute(x, axes, [(i, i ^ bits) for i in range(size)])


def after(x, y):
    return lax.optimization_barrier((x, y))[0]


def merge(parts):
    top = parts[0][..., 0, :]
    for part in parts[1:]:
        top = jnp.maximum(top, part[..., 0, :])
    totals = [part[..., 1, :] * jnp.exp(part[..., 0, :] - top) for part in parts]
    hits = [part[..., 2, :] for part in parts]
    while len(totals) > 1:
        half = len(totals) // 2
        totals = [totals[i] + totals[i + half] for i in range(half)]
        hits = [hits[i] + hits[i + half] for i in range(half)]
    return jnp.stack([top, totals[0], hits[0]], axis=-2)


def swap(x, axis):
    return lax.all_to_all(x, axis, 0, 0, tiled=True)


def spread(x, axis):
    return swap(jnp.broadcast_to(x[None], (lax.axis_size(axis),) + x.shape), axis)


def pick(pieces, index):
    return lax.dynamic_index_in_dim(jnp.stack(pieces), index, 0, keepdims=False)


def total(pieces):
    pieces = [pieces[i].astype(F32) for i in range(4)]
    return (pieces[0] + pieces[2]) + (pieces[1] + pieces[3])


def local(hidden_parts, targets, norm_gain, head_weight):
    s, y, h, c, t = (lax.axis_index(name) for name in ("s", "y", "h", "c", "t"))
    me = 2 * h + c
    rows, cols = head_weight.shape
    part = cols // 4
    width = 4 * rows
    batches, tok_count, features = hidden_parts.shape[1:]
    count = batches * tok_count
    size = count // CHUNKS
    quarter = size // 4
    eighth = quarter // 2

    pieces = [lax.dynamic_slice_in_dim(head_weight, (me ^ r) * part, part, 1) for r in range(4)]
    early = 3 * rows // 4
    arrived = [pieces[0], flip(pieces[1], ("h", "c"), 1)]
    first = flip(pieces[2][:early], ("h", "c"), 2)
    first_column = (me + 4 * (4 * s + t)) * part

    hidden = hidden_parts.reshape(CHUNKS, 4, quarter, features)
    own = lax.dynamic_index_in_dim(hidden, t, 1, keepdims=False).reshape(CHUNKS * quarter, features)
    mixed = own.astype(F32) + flip(own, ("s",), 1).astype(F32)
    radius = jnp.sqrt(jnp.mean(mixed * mixed, axis=-1, keepdims=True) + NORM_EPS)
    unit = mixed / radius
    normed = (norm_gain * unit).astype(BF16)
    over_y = swap(normed.reshape(CHUNKS * quarter, 4, width).transpose(1, 0, 2), "y")
    got = flip(after(over_y, first), ("s", "h"), 3)
    second = flip(after(pieces[2][early:], got), ("h", "c"), 2)
    arrived.append(jnp.concatenate([first, second]))
    arrived.append(flip(after(pieces[3], second), ("h", "c"), 3))
    blocks = jnp.stack(arrived)
    weight = jnp.concatenate([lax.dynamic_index_in_dim(blocks, me ^ a, 0, keepdims=False) for a in range(4)], axis=0)
    over_h = jnp.stack([v.reshape(4, CHUNKS, quarter, width).transpose(1, 0, 2, 3) for v in (over_y, got)], axis=2)
    over_t = spread(over_h, "t")
    unit = unit.reshape(CHUNKS, 2, eighth, features)
    radius = radius.reshape(CHUNKS, 2, eighth, 1)

    ids = after(targets.reshape(count), got)
    ids = jnp.stack([ids, flip(ids, ("h",), 1)])
    ids = jnp.stack([ids, flip(ids, ("c",), 1)])

    def gather(over_t):
        over_c = jnp.stack([over_t, flip(over_t, ("c",), 1)]).transpose(2, 0, 1, 3, 4, 5)
        return lax.optimization_barrier(over_c.reshape(16 * size, width))

    def partial_logits(gathered):
        out = jnp.dot(gathered, weight, preferred_element_type=F32).astype(F16).reshape(4, 4 * size, part)
        return out, swap(out, "y")

    def statistics(k, pieces):
        logits = total(pieces)
        here = ids.reshape(2, 2, CHUNKS, 4, quarter)[:, :, k].transpose(0, 2, 1, 3).reshape(-1)
        is_target = lax.broadcasted_iota(jnp.int32, logits.shape, 1) == (here - first_column)[:, None]
        top = jnp.max(logits, axis=1)
        sums = jnp.sum(jnp.exp(logits - top[:, None]), axis=1)
        hit = jnp.sum(jnp.where(is_target, logits, 0.0), axis=1)
        stats = jnp.stack([v.reshape(2, 4, 2, quarter) for v in (top, sums, hit)], axis=3)
        stats = merge([stats, flip(stats, ("c",), 1)[::-1]])
        got = [flip(stats, ("s", "h"), r) for r in range(1, 4)]
        stats = merge([stats, got[0][:, :, ::-1], got[1], got[2][:, :, ::-1]])
        return logits, is_target, stats

    def loss_and_grad(logits, is_target, stats):
        stats = merge([stats] + [shift(stats, "t", r) for r in range(1, 4)])
        log_total = stats[..., 0, :] + jnp.log(stats[..., 1, :])
        loss = log_total - stats[..., 2, :]
        grad = (jnp.exp(logits - log_total.reshape(-1)[:, None]) - is_target.astype(F32)).astype(BF16)
        return loss[0, :, 0].reshape(size), grad

    def row_product(grads):
        ordered = grads.reshape(4, 2, 4, 2 * quarter, part).transpose(1, 2, 0, 3, 4).reshape(16 * size, part)
        product = lax.dot_general(ordered, weight, (((1,), (1,)), ((), ())), preferred_element_type=F32)
        return lax.optimization_barrier((product * ROW_SCALE).astype(F16).reshape(2, 8 * size, width))

    def head_product(gathered, grads):
        return lax.dot_general(gathered, grads, (((0,), (0,)), ((), ())), preferred_element_type=F32)

    def over_cores(products):
        kept, sent = products
        kept = (kept.astype(F32) + flip(sent, ("c",), 1).astype(F32)).astype(F16)
        return kept.reshape(4, 4, 2 * quarter, width)

    def to_places(pieces, index, axis):
        sent = [lax.dynamic_index_in_dim(pieces, (index + r) % 4, 0, keepdims=False) for r in range(4)]
        return [sent[0]] + [shift(sent[4 - r], axis, r) for r in range(1, 4)]

    def over_z(pieces):
        kept = total(pieces).reshape(4, 2, 2, eighth, width)
        mine = lax.dynamic_index_in_dim(kept, s, 2, keepdims=False)
        other = lax.dynamic_index_in_dim(kept, 1 - s, 2, keepdims=False).astype(F16)
        got = [
            flip(mine[:, 1].astype(F16), ("s", "h"), 1),
            flip(other[:, 0], ("s", "h"), 2),
            flip(other[:, 1], ("s", "h"), 3),
        ]
        return (mine[:, 0] + got[0].astype(F32)) + (got[1].astype(F32) + got[2].astype(F32)), got

    def to_owner(k, summed):
        blocks = to_places(summed.astype(F16), y, "y")
        row_grads = jnp.concatenate([pick(blocks, (b - y) % 4) for b in range(4)], axis=1).astype(F32) * (1.0 / ROW_SCALE)
        u = lax.dynamic_index_in_dim(unit[k], s, 0, keepdims=False)
        scaled = norm_gain * row_grads
        hidden_grad = scaled - u * jnp.mean(scaled * u, axis=-1, keepdims=True)
        hidden_grad = hidden_grad / lax.dynamic_index_in_dim(radius[k], s, 0, keepdims=False)
        return hidden_grad.astype(BF16), jnp.sum(row_grads * u, axis=0, keepdims=True)

    def in_order(mine, got):
        return jnp.stack([pick([mine, got], a ^ s) for a in range(2)]).reshape(quarter, features)

    def halves(v):
        upper = v.astype(BF16)
        return [upper, (v - upper.astype(F32)).astype(BF16)]

    def whole(rows):
        return rows[-2:-1].astype(F32) + rows[-1:].astype(F32)

    first_rows, ids = lax.optimization_barrier((over_t[:, 0], ids))
    rows_here = gather(after(first_rows, arrived[3]))
    _, got = partial_logits(rows_here)
    token_loss, grad = loss_and_grad(*statistics(0, got))
    grads = spread(grad, "y").reshape(16 * size, part)

    products = row_product(grads)
    got_t = swap(over_cores(products), "t")
    head = head_product(rows_here, after(grads, products))
    head = (head * HEAD_SCALE).astype(F16).reshape(4, rows, part)
    got_head = [lax.dynamic_index_in_dim(head, me ^ r, 0, keepdims=False) for r in range(4)]
    got_head = [got_head[0]] + [flip(got_head[r], ("h", "c"), r) for r in range(1, 4)]
    summed, _ = over_z(after(got_t, got_head[2:]))
    hid1, gain1 = to_owner(0, summed)

    sent1 = jnp.concatenate([hid1] + halves(gain1), axis=0)
    pair1 = flip(sent1, ("s",), 1)
    whole1 = in_order(hid1, pair1[:eighth])
    whole1 = jnp.concatenate([whole1] + halves(whole(sent1) + whole(pair1)), axis=0)
    all1 = [whole1] + [shift(whole1, "t", r) for r in range(1, 4)]
    gain = (whole(all1[0]) + whole(all1[2])) + (whole(all1[1]) + whole(all1[3]))
    all1 = jnp.concatenate([pick([v[:quarter] for v in all1], (a - t) % 4) for a in range(4)], axis=0)

    head_grad = jnp.zeros((rows, cols), F32)
    for r in range(4):
        piece = after(got_head[r], pair1).astype(F32) * (1.0 / HEAD_SCALE)
        head_grad = lax.dynamic_update_slice(head_grad, piece, (0, (me ^ r) * part))
    token_loss = token_loss.reshape(batches, tok_count)
    hidden_grad = all1.astype(F32)
    return token_loss, hidden_grad.reshape(1, batches, tok_count, features), head_grad, gain


def solution(mesh):
    fine = Mesh(mesh.devices.reshape(2, 4, 2, 2, 4), ("s", "y", "h", "c", "t"))
    dp = ("y", "h", "c")
    in_specs = (P("s", None, dp, None), P(None, dp), P(), P(dp, ("s", "t")))
    out_specs = (P(None, dp), P("s", None, dp, None), P(dp, ("s", "t")), P(dp, None))
    return jax.shard_map(local, mesh=fine, in_specs=in_specs, out_specs=out_specs, check_vma=False)
```

```python
import jax
import jax.numpy as jnp
from jax import lax
from jax.sharding import Mesh, PartitionSpec as P

NORM_EPS = 1e-05
CHUNKS = 2
ROW_SCALE = 2.0**17
HEAD_SCALE = 2.0**-3
BF16, F16, F32 = jnp.bfloat16, jnp.float16, jnp.float32


def shift(x, axis, step):
    size = lax.axis_size(axis)
    return lax.ppermute(x, axis, [((i + step) % size, i) for i in range(size)])


def flip(x, axes, bits):
    size = 1
    for axis in axes:
        size *= lax.axis_size(axis)
    return lax.ppermute(x, axes, [(i, i ^ bits) for i in range(size)])


def after(x, y):
    return lax.optimization_barrier((x, y))[0]


def pick(pieces, index):
    return lax.dynamic_index_in_dim(jnp.stack(pieces), index, 0, keepdims=False)


def merge(parts):
    top = parts[0][..., 0, :]
    for part in parts[1:]:
        top = jnp.maximum(top, part[..., 0, :])
    totals = [part[..., 1, :] * jnp.exp(part[..., 0, :] - top) for part in parts]
    hits = [part[..., 2, :] for part in parts]
    while len(totals) > 1:
        half = len(totals) // 2
        totals = [totals[i] + totals[i + half] for i in range(half)]
        hits = [hits[i] + hits[i + half] for i in range(half)]
    return jnp.stack([top, totals[0], hits[0]], axis=-2)


def local(hidden_parts, targets, norm_gain, head_weight):
    s, y, h, c, t = (lax.axis_index(name) for name in ("s", "y", "h", "c", "t"))
    me = 2 * h + c
    rows, cols = head_weight.shape
    part = cols // 4
    width = 4 * rows
    batches, tok_count, features = hidden_parts.shape[1:]
    count = batches * tok_count
    size = count // CHUNKS
    quarter = size // 4
    eighth = quarter // 2

    pieces = [lax.dynamic_slice_in_dim(head_weight, (me ^ r) * part, part, 1) for r in range(4)]
    arrived = [pieces[0], flip(pieces[1], ("h", "c"), 1), flip(pieces[2], ("h", "c"), 2)]
    first_column = (me + 4 * (4 * s + t)) * part

    hidden = hidden_parts.reshape(CHUNKS, 4, quarter, features)
    own = lax.dynamic_index_in_dim(hidden, t, 1, keepdims=False).reshape(CHUNKS * quarter, features)
    mixed = own.astype(F32) + flip(own, ("s",), 1).astype(F32)
    radius = jnp.sqrt(jnp.mean(mixed * mixed, axis=-1, keepdims=True) + NORM_EPS)
    unit = mixed / radius
    normed = (norm_gain * unit).astype(BF16)
    sent = [lax.dynamic_slice_in_dim(normed, ((y + r) % 4) * width, width, 1) for r in range(4)]
    over_y = [sent[0]] + [shift(sent[4 - r], "y", r) for r in range(1, 4)]
    over_y = jnp.stack([v.reshape(CHUNKS, quarter, width) for v in over_y], axis=1)
    got = flip(after(over_y, arrived[2]), ("s", "h"), 3)
    over_h = jnp.stack([over_y, got], axis=2)
    arrived.append(flip(after(pieces[3], got), ("h", "c"), 3))
    weight = jnp.concatenate([pick(arrived, me ^ a) for a in range(4)], axis=0)
    unit = unit.reshape(CHUNKS, 2, eighth, features)
    radius = radius.reshape(CHUNKS, 2, eighth, 1)

    ids = after(targets.reshape(count), over_y)
    ids = jnp.stack([ids, flip(ids, ("h",), 1)])
    ids = [ids, flip(ids, ("c",), 1)]

    def gather(k, wait):
        got = after([shift(over_h[k], "t", r) for r in range(1, 4)], wait)
        over_t = jnp.stack([over_h[k]] + got, axis=1)
        over_c = jnp.stack([over_t, flip(over_t, ("c",), 1)], axis=1)
        return over_c.reshape(4, 4 * size, width)

    def partial_logits(gathered):
        out = {r: jnp.dot(gathered[r], weight, preferred_element_type=F32).astype(F16) for r in (2, 1, 3)}
        own = jnp.dot(gathered[0], weight, preferred_element_type=F32)
        return own, {r: shift(out[4 - r], "y", r) for r in (2, 1, 3)}, [out[r] for r in (1, 2, 3)]

    def chunk_ids(k):
        listed = []
        for rc in range(2):
            per_h = [ids[rc][rh].reshape(CHUNKS, 4, quarter)[k] for rh in range(2)]
            for rt in range(4):
                for rh in range(2):
                    listed.append(lax.dynamic_index_in_dim(per_h[rh], (t + rt) % 4, 0, keepdims=False))
        return jnp.concatenate(listed)

    def loss_and_grad(k, own, got, before_last):
        logits = (own + got[2].astype(F32)) + (got[1].astype(F32) + got[3].astype(F32))
        is_target = lax.broadcasted_iota(jnp.int32, logits.shape, 1) == (chunk_ids(k) - first_column)[:, None]
        top = jnp.max(logits, axis=1)
        total = jnp.sum(jnp.exp(logits - top[:, None]), axis=1)
        hit = jnp.sum(jnp.where(is_target, logits, 0.0), axis=1)
        stats = jnp.stack([v.reshape(2, 4, 2, quarter) for v in (top, total, hit)], axis=3)
        stats = merge([stats, flip(stats, ("c",), 1)[::-1]])
        got = [flip(stats, ("s", "h"), r) for r in range(1, 4)]
        stats = merge([stats, got[0][:, :, ::-1], got[1], got[2][:, :, ::-1]])
        if before_last is not None:
            stats = after(stats, before_last)
        stats = merge([stats] + [jnp.roll(shift(stats, "t", r), r, axis=1) for r in range(1, 4)])
        log_total = stats[..., 0, :] + jnp.log(stats[..., 1, :])
        loss = log_total - stats[..., 2, :]
        log_total = log_total.reshape(-1)
        grad = (jnp.exp(logits - log_total[:, None]) - is_target.astype(F32)).astype(BF16)
        own = loss[0, :, 0]
        own = jnp.concatenate([lax.dynamic_index_in_dim(own, (a - t) % 4, 0, keepdims=False) for a in range(4)])
        return own, [grad] + [shift(grad, "y", r) for r in range(1, 4)]

    def row_products(grads):
        return [
            lax.dot_general(g, weight, (((1,), (1,)), ((), ())), preferred_element_type=F32) * ROW_SCALE
            for g in grads
        ]

    def head_product(gathered, grads):
        return lax.dot_general(
            gathered.reshape(-1, width),
            jnp.concatenate(grads, axis=0),
            (((0,), (0,)), ((), ())),
            preferred_element_type=F32,
        )

    def over_cores(products, wait):
        half = products[0].shape[0] // 2
        sent = jnp.stack([p[half:].astype(F16) for p in products])
        got = flip(after(sent, wait), ("c",), 1)
        kept = jnp.stack([p[:half] for p in products]) + got.astype(F32)
        return kept.reshape(4, 4, 2 * quarter, width)

    def over_tensor(kept):
        sent = kept[:, 1:].astype(F16)
        got = [shift(sent[:, 3 - r], "t", r) for r in range(1, 4)]
        kept = (kept[:, 0] + got[1].astype(F32)) + (got[0].astype(F32) + got[2].astype(F32))
        return kept.reshape(4, 2, 2, eighth, width), got

    def over_z(kept):
        mine = lax.dynamic_index_in_dim(kept, s, 2, keepdims=False)
        other = lax.dynamic_index_in_dim(kept, 1 - s, 2, keepdims=False).astype(F16)
        got = [
            flip(mine[:, 1].astype(F16), ("s", "h"), 1),
            flip(other[:, 0], ("s", "h"), 2),
            flip(other[:, 1], ("s", "h"), 3),
        ]
        return (mine[:, 0] + got[0].astype(F32)) + (got[1].astype(F32) + got[2].astype(F32)), got

    def to_owner(k, summed):
        sent = summed.astype(F16)
        got = [shift(sent[4 - r], "y", r) for r in range(1, 4)]
        blocks = [summed[0]] + [g.astype(F32) for g in got]
        row_grads = jnp.concatenate([pick(blocks, (b - y) % 4) for b in range(4)], axis=1) * (1.0 / ROW_SCALE)
        u = lax.dynamic_index_in_dim(unit[k], s, 0, keepdims=False)
        scaled = norm_gain * row_grads
        hidden_grad = scaled - u * jnp.mean(scaled * u, axis=-1, keepdims=True)
        hidden_grad = hidden_grad / lax.dynamic_index_in_dim(radius[k], s, 0, keepdims=False)
        return hidden_grad.astype(BF16), jnp.sum(row_grads * u, axis=0, keepdims=True), got

    def in_order(mine, got):
        return jnp.stack([pick([mine, got], a ^ s) for a in range(2)]).reshape(quarter, features)

    def all_rows(pieces):
        return jnp.concatenate([pick(pieces, (a - t) % 4) for a in range(4)], axis=0).astype(F32)

    def halves(v):
        upper = v.astype(BF16)
        return [upper, (v - upper.astype(F32)).astype(BF16)]

    def whole(rows):
        return rows[-2:-1].astype(F32) + rows[-1:].astype(F32)

    x0 = gather(0, arrived[3])
    own0, got0, last0 = partial_logits(x0)
    x1 = gather(1, last0)
    own1, got1, last1 = partial_logits(x1)
    loss0, grads0 = loss_and_grad(0, after(own0, last1), got0, None)
    loss1, grads1 = loss_and_grad(1, after(own1, grads0[0]), got1, grads0[1])

    rows0, got_t0 = over_tensor(over_cores(row_products(grads0), last1))
    head0 = head_product(x0, after(grads0, grads1[0]))
    summed0, got_z0 = over_z(rows0)
    hid0, gain0, got_y0 = to_owner(0, summed0)
    pair0 = flip(hid0, ("s",), 1)

    grads1 = after(grads1, (head0, got_t0))
    head = (head0 + head_product(x1, grads1)).reshape(4, rows, part)
    pieces = [lax.dynamic_index_in_dim(head, me ^ r, 0, keepdims=False) for r in range(4)]
    sent = [None] + [(piece * HEAD_SCALE).astype(F16) for piece in pieces[1:]]
    got_head = [pieces[0]] + [flip(after(sent[r], pair0), ("h", "c"), r) for r in range(1, 4)]
    kept1 = over_cores(row_products(after(grads1, (sent[2:], got_z0))), got_y0)
    rows1, got_t1 = over_tensor(kept1)
    whole0 = after(in_order(hid0, pair0), got_t1)
    all0 = [whole0] + [shift(whole0, "t", r) for r in range(1, 4)]
    out0 = all_rows(all0)
    hid1, gain1, _ = to_owner(1, over_z(after(rows1, (got_head[2:], all0[1:])))[0])

    sent1 = jnp.concatenate([hid1] + halves(gain0 + gain1), axis=0)
    pair1 = flip(sent1, ("s",), 1)
    whole1 = in_order(hid1, pair1[:eighth])
    whole1 = jnp.concatenate([whole1] + halves(whole(sent1) + whole(pair1)), axis=0)
    all1 = [whole1] + [shift(whole1, "t", r) for r in range(1, 4)]
    out1 = all_rows([v[:quarter] for v in all1])
    gain = (whole(all1[0]) + whole(all1[2])) + (whole(all1[1]) + whole(all1[3]))

    head_grad = jnp.zeros((rows, cols), F32)
    for r in range(4):
        piece = got_head[r]
        if r:
            piece = after(piece, pair1).astype(F32) * (1.0 / HEAD_SCALE)
        head_grad = lax.dynamic_update_slice(head_grad, piece, (0, (me ^ r) * part))

    token_loss = jnp.concatenate([loss0, loss1]).reshape(batches, tok_count)
    hidden_grad = jnp.concatenate([out0, out1]).reshape(1, batches, tok_count, features)
    return token_loss, hidden_grad, head_grad, gain


def solution(mesh):
    fine = Mesh(mesh.devices.reshape(2, 4, 2, 2, 4), ("s", "y", "h", "c", "t"))
    dp = ("y", "h", "c")
    in_specs = (P("s", None, dp, None), P(None, dp), P(), P(dp, ("s", "t")))
    out_specs = (P(None, dp), P("s", None, dp, None), P(dp, ("s", "t")), P(dp, None))
    return jax.shard_map(local, mesh=fine, in_specs=in_specs, out_specs=out_specs, check_vma=False)
```
